32 devices in a mesh: member: 2 (over x), seq: 4 (over z), head: 4 (over y, core).
Axes of the slice: x: 2, y: 2, z: 4, core: 2. Of those that a mesh axis runs over, the one named last changes fastest.
Arguments:
- tokens: bfloat16 [2048, 5120], P(('seq', 'head')), may hold values from -6 to 6
- lattice: int32 [3, 2048], P(None, 'seq'), may hold values from 0 to 63
- timestep: int32 [4], replicated, may hold values from 0 to 999
- time_weight: bfloat16 [2, 256, 5120], P(None, None, 'seq'), may hold values from -0.375 to 0.375
- query_weight: bfloat16 [2, 5120, 2560], P('member', 'seq', 'head'), may hold values from -6 to 6
- key_weight: bfloat16 [5120, 2560], P('seq', 'head'), may hold values from -6 to 6
- values: bfloat16 [2048, 2560], P(('seq', 'head')), may hold values from -6 to 6
- cotangent: bfloat16 [2, 2048, 2560], P('member', ('seq', 'head')), may hold values from -72 to 72
Outputs:
- fisher: float32 [2, 5120, 2560], P('member', 'seq', 'head')
- merged: float32 [5120, 2560], P('seq', 'head')
The draws below stay inside these ranges and needn't reach their ends.
All inputs are finite; a program needn't handle non-finite values.
Results may differ from the reference program's by a relative error of at most 0.022.
Values may be sent and summed in bfloat16 or wider, within the bound.
No kernel may reach another device: no remote copies, remote signals or barrier semaphores. Data moves between devices by JAX's collectives and lax.ppermute only.
A program may use at most 128 MiB of HBM per device.

```python
import math
import jax
import jax.numpy as jnp
from jax import lax

D = 5120
HEAD_SIZE = 128
FREQ = 256
CLIPS = 4
TOKENS = 2048
ATTN = 2560
MEMBERS = 2


def touch_ends(result, own_key, least, largest):
    place = [jax.random.randint(jax.random.fold_in(own_key, axis), (), 0, length) for axis, length in enumerate(result.shape)]
    main_axis = result.shape.index(max(result.shape))
    neighbour = place[:main_axis] + [(place[main_axis] + 1) % result.shape[main_axis]] + place[main_axis + 1:]
    return result.at[tuple(place)].set(least).at[tuple(neighbour)].set(largest)


def strengthened(result, rng, source, target, blocks, factor):
    def block_of(axis_at):
        return (jnp.arange(result.shape[axis_at]) // (result.shape[axis_at] // blocks)).reshape((-1,) + (1,) * (result.ndim - 1 - axis_at))

    one_side = jax.random.permutation(rng, blocks)[block_of(target)]
    far = (block_of(target) + blocks // 2) % blocks
    return jnp.where((block_of(source) == one_side) | (block_of(source) == far), factor * result, result)


def steps_of(own_key, shape, shards, smallest, high):
    loudness, own = 1.0, jax.random.fold_in(own_key, 6)
    for dim, blocks in shards:
        steps = jnp.exp(jax.random.uniform(jax.random.fold_in(own, dim), (blocks,), jnp.float32, smallest / len(shards), high / len(shards)))
        loudness = loudness * jnp.repeat(steps, shape[dim] // blocks).reshape([-1 if axis == dim else 1 for axis in range(len(shape))])
    return loudness


def noise(own_key, extent, scale, most, pieces=(), dtype=jnp.bfloat16):
    loudness = steps_of(own_key, extent, pieces, -0.22, 0.18) if pieces else 1.0
    array = jax.random.normal(own_key, extent, jnp.float32) * scale * loudness
    return jnp.minimum(jnp.maximum(array, -most), most).astype(dtype)


def noise_with(own_key, shape, scale, limit, split, heavy, kind=jnp.bfloat16):
    result = scale * jax.random.normal(own_key, shape, jnp.float32)
    if split:
        result = result * steps_of(own_key, shape, split, -0.22, 0.18)
    return jnp.clip(strengthened(result, jax.random.fold_in(own_key, 3), *heavy), -limit, limit).astype(kind)


def setup_inputs(seed: int = 0) -> dict:
    arg_keys = jax.random.split(jax.random.key(seed), 9)
    tokens = noise_with(arg_keys[0], (TOKENS, D), 1.0, 6.0, ((0, 16),), (0, 1, 16, 2.0))
    lattice = touch_ends(jax.random.randint(arg_keys[1], (3, TOKENS), 0, 64), jax.random.fold_in(arg_keys[1], 1), 0, 63).astype(jnp.int32)
    timestep = touch_ends(jax.random.randint(arg_keys[2], (CLIPS,), 0, 1000), jax.random.fold_in(arg_keys[2], 1), 0, 999).astype(jnp.int32)
    time_weight = noise(arg_keys[3], (2, FREQ, D), FREQ ** -0.5, 0.375, ((2, 4),))
    query_weight = noise(arg_keys[4], (MEMBERS, D, ATTN), 1.0, 6.0, ((0, 2), (1, 4), (2, 4)))
    key_weight = noise(arg_keys[5], (D, ATTN), 1.0, 6.0, ((0, 4), (1, 4)))
    values = noise(arg_keys[6], (TOKENS, ATTN), 1.0, 6.0, ((0, 16),))
    cotangent = noise(arg_keys[7], (MEMBERS, TOKENS, ATTN), 12.0, 72.0, ((0, 2), (1, 16)))
    return {"tokens": tokens, "lattice": lattice, "timestep": timestep, "time_weight": time_weight, "query_weight": query_weight, "key_weight": key_weight, "values": values, "cotangent": cotangent}


damping = 0.01

def time_features(timestep, feature_count):
    halfway = feature_count // 2
    ladder = jnp.arange(halfway).astype(jnp.float32)
    frequency = jnp.exp(-math.log(10000.0) * 2.0 * ladder / feature_count)
    angles = timestep.astype(jnp.float32)[:, None] * frequency[None, :]
    return jnp.concatenate([jnp.cos(angles), jnp.sin(angles)], axis=1).astype(jnp.bfloat16)

def rope_tables(lattice, head_width):
    halfway = head_width // 2
    side_pairs = head_width // 6
    frame_pairs = halfway - 2 * side_pairs
    column = jnp.arange(head_width)
    pair_index = column % halfway
    which_axis = jnp.where(pair_index < frame_pairs, 0, jnp.where(pair_index < frame_pairs + side_pairs, 1, 2))
    anchor = jnp.where(which_axis == 0, 0, jnp.where(which_axis == 1, frame_pairs, frame_pairs + side_pairs))
    pair_span = jnp.where(which_axis == 0, frame_pairs, side_pairs)
    frequency = jnp.exp(-math.log(10000.0) * (pair_index - anchor).astype(jnp.float32) / pair_span.astype(jnp.float32))
    position = lattice.astype(jnp.float32)
    angles = jnp.zeros((lattice.shape[1], head_width), jnp.float32)
    for axis_number in range(3):
        chosen = jnp.where(which_axis == axis_number, frequency, 0.0)
        angles = angles + position[axis_number][:, None] * chosen[None, :]
    sign_flip = jnp.where(column < halfway, -1.0, 1.0).astype(jnp.float32)
    return (jnp.cos(angles), jnp.sin(angles) * sign_flip[None, :])

def normed_rotation(stacked, cosine, sine_table):
    halfway = stacked.shape[2] // 2
    inverse = lax.rsqrt(lax.optimization_barrier(jnp.mean(stacked * stacked, axis=2, keepdims=True)) + 1e-06)
    normed = stacked * inverse
    rotated = normed * cosine[:, None, :] + jnp.roll(normed, halfway, axis=2) * sine_table[:, None, :]
    return (normed, inverse, rotated)

def attention_backward(query_pre, key_pre, values, cotangent, cosine, sine_table, head_width):
    length, width = query_pre.shape
    head_count = width // head_width
    halfway = head_width // 2
    query_normed, query_inverse, query_rotated = normed_rotation(query_pre.reshape(length, head_count, head_width), cosine, sine_table)
    unused_normed, unused_inverse, key_rotated = normed_rotation(key_pre.reshape(length, head_count, head_width), cosine, sine_table)
    query_round = query_rotated.astype(jnp.bfloat16)
    key_wide = key_rotated.astype(jnp.bfloat16).astype(jnp.float32)
    value_heads = values.reshape(length, head_count, head_width).astype(jnp.float32)
    block_rows = min(length, 512)
    block_count = length // block_rows
    score_scale = head_width ** (-0.5)

    def one_block(portion):
        query_block, grad_block = portion
        grad_wide = grad_block.astype(jnp.float32)
        scores = jnp.einsum('qhd,khd->hqk', query_block.astype(jnp.float32), key_wide) * score_scale
        raised = jnp.exp(scores)
        weights = raised / lax.optimization_barrier(jnp.sum(raised, axis=2, keepdims=True))
        rounded = weights.astype(jnp.bfloat16)
        attended = jnp.einsum('hqk,khd->qhd', rounded.astype(jnp.float32), value_heads)
        inner = lax.optimization_barrier(jnp.sum(grad_wide * attended, axis=2))
        grad_weights = jnp.einsum('qhd,khd->hqk', grad_wide, value_heads)
        grad_scores = (weights * (grad_weights - inner.T[:, :, None])).astype(jnp.bfloat16)
        return jnp.einsum('hqk,khd->qhd', grad_scores.astype(jnp.float32), key_wide) * score_scale
    grad_rotated = lax.map(one_block, (query_round.reshape(block_count, block_rows, head_count, head_width), cotangent.reshape(block_count, block_rows, head_count, head_width)))
    grad_rotated = grad_rotated.reshape(length, head_count, head_width)
    grad_normed = grad_rotated * cosine[:, None, :] + jnp.roll(grad_rotated * sine_table[:, None, :], halfway, axis=2)
    grad_query = query_inverse * (grad_normed - query_normed * lax.optimization_barrier(jnp.mean(grad_normed * query_normed, axis=2, keepdims=True)))
    return grad_query.reshape(length, width).astype(jnp.bfloat16)

def reference(tokens, lattice, timestep, time_weight, query_weight, key_weight, values, cotangent):
    model_width = tokens.shape[1]
    clip_count = timestep.shape[0]
    clip_length = tokens.shape[0] // clip_count
    attn_width = key_weight.shape[1]
    features = time_features(timestep, time_weight.shape[1])
    modulation = jnp.einsum('cf,jfd->cjd', features.astype(jnp.float32), time_weight.astype(jnp.float32))
    hidden = tokens.astype(jnp.float32).reshape(clip_count, clip_length, model_width)
    average = lax.optimization_barrier(jnp.mean(hidden, axis=2, keepdims=True))
    centred = hidden - average
    variance = lax.optimization_barrier(jnp.mean(centred * centred, axis=2, keepdims=True))
    normed = centred * lax.rsqrt(variance + 1e-06)
    modulated = (normed * (1.0 + modulation[:, 1][:, None, :]) + modulation[:, 0][:, None, :]).astype(jnp.bfloat16)
    lattices = lattice.reshape(3, clip_count, clip_length).transpose(1, 0, 2)
    value_clips = values.reshape(clip_count, clip_length, attn_width)
    results = []
    for member in range(query_weight.shape[0]):
        own_query = query_weight[member]
        cot_clips = cotangent[member].reshape(clip_count, clip_length, attn_width)

        def step(running, portion):
            rows, grid_rows, value_rows, cot_rows = portion
            cosine, sine_table = rope_tables(grid_rows, HEAD_SIZE)
            query_pre = jnp.dot(rows, own_query, preferred_element_type=jnp.float32)
            key_pre = jnp.dot(rows, key_weight, preferred_element_type=jnp.float32)
            grad_query = attention_backward(query_pre, key_pre, value_rows, cot_rows, cosine, sine_table, HEAD_SIZE)
            grad = lax.dot_general(rows, grad_query, (((0,), (0,)), ((), ())), preferred_element_type=jnp.float32)
            squared = lax.optimization_barrier((grad * grad).astype(jnp.bfloat16))
            return (running + squared.astype(jnp.float32), None)
        running, unused_out = lax.scan(step, jnp.zeros((model_width, attn_width), jnp.float32), (modulated, lattices, value_clips, cot_clips))
        results.append(running)
    fisher = jnp.stack(results, axis=0)
    weighted = fisher + damping
    merged = lax.optimization_barrier(jnp.sum(weighted * query_weight.astype(jnp.float32), axis=0)) / lax.optimization_barrier(jnp.sum(weighted, axis=0))
    return (fisher, merged)
```

```python
import functools
import math

import jax
import jax.numpy as jnp
from jax import lax
from jax.experimental import pallas as pl
from jax.experimental.pallas import tpu as pltpu
from jax.sharding import PartitionSpec as P

HEAD_SIZE = 128
damping = 0.01
VMEM_BYTES = 56 * 1024 * 1024


def time_features(timestep, feature_count):
    halfway = feature_count // 2
    ladder = jnp.arange(halfway).astype(jnp.float32)
    frequency = jnp.exp(-math.log(10000.0) * 2.0 * ladder / feature_count)
    angles = timestep.astype(jnp.float32)[:, None] * frequency[None, :]
    return jnp.concatenate([jnp.cos(angles), jnp.sin(angles)], axis=1).astype(jnp.bfloat16)


def rope_tables(lattice, head_width):
    halfway = head_width // 2
    side_pairs = head_width // 6
    frame_pairs = halfway - 2 * side_pairs
    column = jnp.arange(head_width)
    pair_index = column % halfway
    which_axis = jnp.where(
        pair_index < frame_pairs, 0, jnp.where(pair_index < frame_pairs + side_pairs, 1, 2)
    )
    anchor = jnp.where(
        which_axis == 0, 0, jnp.where(which_axis == 1, frame_pairs, frame_pairs + side_pairs)
    )
    pair_span = jnp.where(which_axis == 0, frame_pairs, side_pairs)
    frequency = jnp.exp(
        -math.log(10000.0)
        * (pair_index - anchor).astype(jnp.float32)
        / pair_span.astype(jnp.float32)
    )
    position = lattice.astype(jnp.float32)
    angles = jnp.zeros((lattice.shape[1], head_width), jnp.float32)
    for axis_number in range(3):
        chosen = jnp.where(which_axis == axis_number, frequency, 0.0)
        angles = angles + position[axis_number][:, None] * chosen[None, :]
    sign_flip = jnp.where(column < halfway, -1.0, 1.0).astype(jnp.float32)
    return (jnp.cos(angles), jnp.sin(angles) * sign_flip[None, :])


def partner(rows):
    return pltpu.roll(rows, rows.shape[1] // 2, 1)


def head_rotation(rows, cosine, sine):
    inverse = lax.rsqrt(jnp.mean(rows * rows, axis=1, keepdims=True) + 1e-06)
    normed = rows * inverse
    return normed, inverse, normed * cosine + partner(normed) * sine


def rotate_kernel(rows_ref, cosine_ref, sine_ref, out_ref):
    out_ref[...] = head_rotation(rows_ref[...], cosine_ref[...], sine_ref[...])[2].astype(
        out_ref.dtype
    )


def rotate_heads(rows, cosine, sine):
    length, width = rows.shape
    column = pl.BlockSpec((length, HEAD_SIZE), lambda j: (0, j))
    table = pl.BlockSpec((length, HEAD_SIZE), lambda j: (0, 0))
    return pl.pallas_call(
        rotate_kernel,
        grid=(width // HEAD_SIZE,),
        in_specs=[column, table, table],
        out_specs=column,
        out_shape=jax.ShapeDtypeStruct((length, width), jnp.bfloat16),
        compiler_params=pltpu.CompilerParams(vmem_limit_bytes=VMEM_BYTES),
        name="rotate_heads",
    )(rows, cosine, sine)


def attention_kernel(query_ref, key_ref, value_ref, cot_ref, cosine_ref, sine_ref, out_ref):
    cosine, sine = cosine_ref[...], sine_ref[...]
    key, value, cot = key_ref[...], value_ref[...], cot_ref[...]
    scale = query_ref.shape[1] ** (-0.5)
    normed, inverse, rotated = head_rotation(query_ref[...], cosine, sine)
    across = (((1,), (1,)), ((), ()))
    scores = lax.dot_general(
        rotated.astype(jnp.bfloat16), key, across, preferred_element_type=jnp.float32
    )
    raised = jnp.exp2(scores * (scale * math.log2(math.e)))
    weights = raised * (1.0 / jnp.sum(raised, axis=1, keepdims=True))
    attended = jnp.dot(weights.astype(jnp.bfloat16), value, preferred_element_type=jnp.float32)
    inner = jnp.sum(cot.astype(jnp.float32) * attended, axis=1, keepdims=True)
    grad_weights = lax.dot_general(cot, value, across, preferred_element_type=jnp.float32)
    grad_scores = (weights * (grad_weights - inner)).astype(jnp.bfloat16)
    grad_rotated = jnp.dot(grad_scores, key, preferred_element_type=jnp.float32) * scale
    grad_normed = grad_rotated * cosine + partner(grad_rotated * sine)
    shared = jnp.mean(grad_normed * normed, axis=1, keepdims=True)
    grad_query = inverse * (grad_normed - normed * shared)
    out_ref[...] = grad_query.T.astype(out_ref.dtype)


def attention_grad(query_pre, key, value, cot, cosine, sine, first, count):
    length = query_pre.shape[0]
    column = pl.BlockSpec((length, HEAD_SIZE), lambda j: (0, j + first))
    table = pl.BlockSpec((length, HEAD_SIZE), lambda j: (0, 0))
    return pl.pallas_call(
        attention_kernel,
        grid=(count,),
        in_specs=[column, column, column, column, table, table],
        out_specs=pl.BlockSpec((HEAD_SIZE, length), lambda j: (j, 0)),
        out_shape=jax.ShapeDtypeStruct((count * HEAD_SIZE, length), jnp.bfloat16),
        compiler_params=pltpu.CompilerParams(vmem_limit_bytes=VMEM_BYTES),
        name="attention_grad",
    )(query_pre, key, value, cot, cosine, sine)


def row_tile(rows):
    return 256 if rows % 256 == 0 else rows


def fisher_kernel(groups, *refs):
    rows, grads, own_ref, low_ref = refs[:groups], refs[groups:-2], refs[-2], refs[-1]

    def squared(clip, grad):
        total, start = 0.0, 0
        for ref in rows:
            block = ref[clip]
            part = grad[:, start : start + block.shape[0]]
            total = total + jnp.dot(part, block, preferred_element_type=jnp.float32)
            start += block.shape[0]
        return total * total

    total = jnp.zeros(own_ref.shape[::-1], jnp.float32)
    clip = 0
    for ref in grads:
        if len(ref.shape) == 2:
            total = total + squared(clip, ref[...])
            clip += 1
        else:
            total = lax.fori_loop(0, ref.shape[0], lambda i, t: t + squared(i, ref[i]), total)
            clip += ref.shape[0]
    fisher = total.T
    own_ref[...] = fisher
    low_ref[...] = fisher.astype(low_ref.dtype)


def drop(kernel, place):
    def run(*refs):
        kernel(*refs[:place], *refs[place + 1 :])

    return run


def in_place(kernel, inputs, specs, previous):
    if previous is None:
        return kernel, inputs, specs, {}
    place = len(inputs)
    return (
        drop(kernel, place),
        list(inputs) + [previous],
        list(specs) + [pl.BlockSpec(memory_space=pl.ANY)],
        {place: 0},
    )


def fisher_rows(rows, grads, first, total_columns, previous):
    width = rows[0].shape[2]
    columns = grads[0].shape[-2]
    tile = row_tile(width)
    specs = [pl.BlockSpec((block.shape[0], block.shape[1], tile), lambda i: (0, 0, i)) for block in rows]
    specs += [pl.BlockSpec(grad.shape, lambda i, n=grad.ndim: (0,) * n) for grad in grads]
    kernel, inputs, specs, aliases = in_place(
        functools.partial(fisher_kernel, len(rows)), [*rows, *grads], specs, previous
    )
    return pl.pallas_call(
        kernel,
        grid=(width // tile,),
        in_specs=specs,
        out_specs=[
            pl.BlockSpec((pl.Element(tile), pl.Element(columns)), lambda i: (i * tile, first)),
            pl.BlockSpec((tile, columns), lambda i: (i, 0)),
        ],
        out_shape=[
            jax.ShapeDtypeStruct((width, total_columns), jnp.float32),
            jax.ShapeDtypeStruct((width, columns), jnp.bfloat16),
        ],
        input_output_aliases=aliases,
        compiler_params=pltpu.CompilerParams(vmem_limit_bytes=VMEM_BYTES),
        name="fisher_rows",
    )(*inputs)


def merge_kernel(here_ref, there_ref, own_ref, other_ref, out_ref):
    zero = lax.axis_index("member") == 0
    here, there = to_f32(here_ref[...]) + damping, to_f32(there_ref[...]) + damping
    one, two = here * to_f32(own_ref[...]), there * to_f32(other_ref[...])
    upper = jnp.where(zero, one, two) + jnp.where(zero, two, one)
    out_ref[...] = upper / (here + there)


def merge_rows(here, there, own_weight, other_weight, first, previous):
    width, columns = here.shape
    tile = row_tile(width)
    plain = pl.BlockSpec((tile, columns), lambda i: (i, 0))
    part = pl.BlockSpec((pl.Element(tile), pl.Element(columns)), lambda i: (i * tile, first))
    kernel, inputs, specs, aliases = in_place(
        merge_kernel, [here, there, own_weight, other_weight], [plain, plain, part, part], previous
    )
    return pl.pallas_call(
        kernel,
        grid=(width // tile,),
        in_specs=specs,
        out_specs=part,
        out_shape=jax.ShapeDtypeStruct(own_weight.shape, jnp.float32),
        input_output_aliases=aliases,
        compiler_params=pltpu.CompilerParams(vmem_limit_bytes=VMEM_BYTES),
        name="merge_rows",
    )(*inputs)


def spread_kernel(place_ref, rows_ref, *outs):
    rows = to_f32(rows_ref[...])
    average = jnp.mean(rows, axis=1, keepdims=True)
    centred = rows - average
    inverse = lax.rsqrt(jnp.mean(centred * centred, axis=1, keepdims=True) + 1e-06)
    size, width = len(outs), outs[0].shape[1]
    for away, out_ref in enumerate(outs):
        start = pl.multiple_of(lax.rem(place_ref[1] + away, size) * width, 128)
        part = to_f32(rows_ref[:, pl.ds(start, width)])
        out_ref[...] = ((part - average) * inverse).astype(out_ref.dtype)


def spread_rows(tokens, member, place, share, size):
    width = tokens.shape[1] // size
    return pl.pallas_call(
        spread_kernel,
        grid_spec=pltpu.PrefetchScalarGridSpec(
            num_scalar_prefetch=1,
            grid=(1,),
            in_specs=[pl.BlockSpec((share, tokens.shape[1]), lambda i, where: (where[0], 0))],
            out_specs=[pl.BlockSpec((share, width), lambda i, where: (0, 0))] * size,
        ),
        out_shape=[jax.ShapeDtypeStruct((share, width), jnp.bfloat16)] * size,
        compiler_params=pltpu.CompilerParams(vmem_limit_bytes=VMEM_BYTES),
        name="spread_rows",
    )(jnp.stack([member, place]).astype(jnp.int32), tokens)


def modulate(rows, modulation):
    return (rows * (1.0 + modulation[1:2]) + modulation[0:1]).astype(jnp.bfloat16)


def project_kernel(pieces, weights, waits, *refs):
    piece_refs, modulation_ref = refs[:pieces], refs[pieces]
    weight_refs = refs[pieces + 1 : pieces + 1 + weights]
    rows_ref, *outs = refs[pieces + 1 + weights + waits :]
    size = rows_ref.shape[0]
    share = piece_refs[0].shape[1]
    order = sorted(range(size), key=lambda away: -min(away, size - away))
    for away in order:
        modulation = modulation_ref[away]
        for i, ref in enumerate(piece_refs):
            rows_ref[away, i * share : (i + 1) * share] = modulate(to_f32(ref[away]), modulation)
        for i, ref in enumerate(weight_refs):
            start = i * pieces * share
            outs[away][start : start + pieces * share] = jnp.dot(
                rows_ref[away], ref[...], preferred_element_type=jnp.float32
            ).astype(outs[away].dtype)


def project_rows(pieces, modulation, weights, waits):
    size, share, width = pieces[0].shape
    length, columns = len(pieces) * share, weights[0].shape[1]
    types = [jnp.bfloat16 if 2 * away == size else jnp.float32 for away in range(size)]
    whole = pl.BlockSpec(memory_space=pltpu.VMEM)
    return pl.pallas_call(
        functools.partial(project_kernel, len(pieces), len(weights), len(waits)),
        in_specs=[whole] * (len(pieces) + 1 + len(weights))
        + [pl.BlockSpec(memory_space=pl.ANY)] * len(waits),
        out_specs=[whole] * (1 + size),
        out_shape=[jax.ShapeDtypeStruct((size, length, width), jnp.bfloat16)]
        + [jax.ShapeDtypeStruct((len(weights) * length, columns), kind) for kind in types],
        compiler_params=pltpu.CompilerParams(vmem_limit_bytes=VMEM_BYTES),
        name="project_rows",
    )(*pieces, modulation, *weights, *waits)


def to_f32(block):
    return block.astype(jnp.float32)


class Ring:
    def __init__(self, size):
        self.size = size
        self.place = lax.axis_index("seq")
        self.short = size <= 8 and size % 2 == 0

    def by_distance(self, blocks):
        return jnp.take(blocks, (self.place - jnp.arange(self.size)) % self.size, axis=0)

    def step(self, block, away):
        pairs = [(i, (i + away) % self.size) for i in range(self.size)]
        return lax.ppermute(block, "seq", pairs)

    def exchange(self, tokens, member, share):
        size = self.size
        width = tokens.shape[1] // size
        if self.short and width % 128 == 0:
            parts = spread_rows(tokens, member, self.place, share, size)
            return jnp.stack(
                list(parts[:1]) + [self.step(part, away) for away, part in enumerate(parts) if away]
            )
        mine = to_f32(lax.dynamic_slice_in_dim(tokens, member * share, share, 0))
        centred = mine - jnp.mean(mine, axis=1, keepdims=True)
        variance = jnp.mean(centred * centred, axis=1, keepdims=True)
        normed = (centred * lax.rsqrt(variance + 1e-06)).astype(jnp.bfloat16)
        parts = normed.reshape(share, size, width)
        return self.by_distance(
            lax.all_to_all(parts, "seq", split_axis=1, concat_axis=0, tiled=False)
        )

    def project(self, pieces, modulation, weights, waits):
        size, half = self.size, self.size // 2
        if not self.short:
            rows = jnp.concatenate(pieces, axis=1)
            rows = jax.vmap(modulate)(to_f32(rows), modulation)
            terms = [
                jnp.einsum("crw,wn->crn", rows, weight, preferred_element_type=jnp.float32)
                for weight in weights
            ]
            terms = jnp.concatenate(terms, axis=1).astype(jnp.bfloat16)
            total = to_f32(lax.psum_scatter(self.by_distance(terms), "seq", tiled=False))
            return rows, total, total
        rows, *terms = project_rows(pieces, modulation, weights, waits)
        middle = terms[0].shape[0] // 2
        right = self.step(terms[half][:middle], 1)
        left = self.step(terms[half][middle:], -1)
        sent = right
        for away in range(half - 1, 0, -1):
            term_right, term_left = terms[size - away], terms[away]
            if away == half - 1:
                term_right = jnp.concatenate(
                    [term_right[:middle] + to_f32(right), term_right[middle:]], axis=0
                )
                term_left = jnp.concatenate(
                    [term_left[:middle], term_left[middle:] + to_f32(left)], axis=0
                )
            else:
                term_right, term_left = term_right + to_f32(right), term_left + to_f32(left)
            sent = term_left.astype(jnp.bfloat16)
            right = self.step(term_right.astype(jnp.bfloat16), 1)
            left = self.step(sent, -1)
        if half == 1:
            total = terms[0] + to_f32(jnp.concatenate([right, left], axis=0))
        else:
            total = terms[0] + to_f32(right) + to_f32(left)
        return rows, total, sent

    def gather(self, block):
        size, half = self.size, self.size // 2
        if not self.short:
            return [self.by_distance(lax.all_gather(block, "seq"))]
        blocks = [None] * size
        blocks[0] = block
        right, left = block, block
        for away in range(1, half):
            right, left = self.step(right, 1), self.step(left, -1)
            blocks[away], blocks[size - away] = right, left
        middle = block.shape[0] // 2
        blocks[half] = jnp.concatenate(
            [self.step(right[:middle], 1), self.step(left[middle:], -1)], axis=0
        )
        return blocks


def on_device(
    axes, tokens, lattice, timestep, time_weight, query_weight, key_weight, values, cotangent
):
    members, clips, heads = axes
    member = lax.axis_index("member")
    clip = lax.axis_index("seq")
    head = lax.axis_index("head")
    own_query = query_weight[0]
    width, columns = own_query.shape
    share = tokens.shape[0] // members

    ring = Ring(clips)

    def x_swap(block):
        return lax.ppermute(block, "member", [(i, i ^ 1) for i in range(members)])

    def h_swap(block, bits):
        return lax.ppermute(block, "head", [(i, i ^ bits) for i in range(heads)])

    own = ring.exchange(tokens, member, share)

    near_y = h_swap(own, 2)
    near_x, far = x_swap(own), x_swap(near_y)

    ordered = timestep[(clip - jnp.arange(clips)) % clips]
    features = time_features(ordered, time_weight.shape[1])
    modulation = jnp.einsum(
        "cf,jfd->cjd", features, time_weight, preferred_element_type=jnp.float32
    )

    def both(block):
        return [block, h_swap(block, 1)]

    rows_near, near, sent = ring.project(
        both(own) + both(near_y), modulation, [own_query, key_weight], []
    )
    rows_far, query_far, _ = ring.project(
        both(near_x) + both(far), modulation, [own_query], [sent]
    )
    rows_here = near.shape[0] // 2
    query_near, key_here = near[:rows_here], near[rows_here:]
    query_pre = jnp.concatenate([query_near, query_far], axis=0)

    grid = lattice.reshape(3, 2, 2, members, share).transpose(0, 3, 1, 2, 4)
    for axis, bit in ((1, member), (2, head // 2), (3, head % 2)):
        grid = jnp.where(bit == 1, jnp.flip(grid, axis), grid)
    cosine, sine = rope_tables(grid.reshape(3, -1), HEAD_SIZE)

    pair = jnp.stack([values, cotangent[0]])
    blocks = []
    for bits in range(heads):
        block = lax.dynamic_slice_in_dim(pair, (head ^ bits) * columns, columns, 2)
        blocks.append(h_swap(block, bits) if bits else block)
    halves = jnp.stack(blocks, axis=1).reshape(2, heads, members, share, columns)
    halves = jnp.concatenate(
        [lax.dynamic_slice_in_dim(halves, member ^ i, 1, 2)[:, :, 0] for i in range(members)], axis=1
    ).reshape(2, members * heads * share, columns)
    value_rows, cot_rows = halves[0], halves[1]

    key_here = rotate_heads(key_here, cosine[:rows_here], sine[:rows_here])
    key_rows = jnp.concatenate([key_here, x_swap(key_here)], axis=0)

    other_query = x_swap(lax.optimization_barrier((own_query, far))[0])

    head_count = columns // HEAD_SIZE
    bounds = [0, (head_count + 1) // 2, head_count]
    fisher, merged = None, None
    for first, last in zip(bounds[:-1], bounds[1:]):
        grad_query = attention_grad(
            query_pre, key_rows, value_rows, cot_rows, cosine, sine, first, last - first
        )
        fisher, low = fisher_rows(
            [rows_near, rows_far], ring.gather(grad_query), first * HEAD_SIZE, columns, fisher
        )
        merged = merge_rows(
            low, x_swap(low), own_query, other_query, first * HEAD_SIZE, merged
        )
    return fisher[None], merged


def solution(mesh):
    axes = (mesh.shape["member"], mesh.shape["seq"], mesh.shape["head"])
    return jax.shard_map(
        functools.partial(on_device, axes),
        mesh=mesh,
        in_specs=(
            P(("seq", "head"), None),
            P(None, "seq"),
            P(),
            P(None, None, "seq"),
            P("member", "seq", "head"),
            P("seq", "head"),
            P(("seq", "head"), None),
            P("member", ("seq", "head"), None),
        ),
        out_specs=(P("member", "seq", "head"), P("seq", "head")),
        check_vma=False,
    )
```

```python
import functools
import math

import jax
import jax.numpy as jnp
from jax import lax
from jax.experimental import pallas as pl
from jax.experimental.pallas import tpu as pltpu
from jax.sharding import PartitionSpec as P

HEAD_SIZE = 128
damping = 0.01
VMEM_BYTES = 24 * 1024 * 1024
FISHER_BYTES = 32 * 1024 * 1024


def time_features(timestep, feature_count):
    halfway = feature_count // 2
    ladder = jnp.arange(halfway).astype(jnp.float32)
    frequency = jnp.exp(-math.log(10000.0) * 2.0 * ladder / feature_count)
    angles = timestep.astype(jnp.float32)[:, None] * frequency[None, :]
    return jnp.concatenate([jnp.cos(angles), jnp.sin(angles)], axis=1).astype(jnp.bfloat16)


def rope_tables(lattice, head_width):
    halfway = head_width // 2
    side_pairs = head_width // 6
    frame_pairs = halfway - 2 * side_pairs
    column = jnp.arange(head_width)
    pair_index = column % halfway
    which_axis = jnp.where(
        pair_index < frame_pairs, 0, jnp.where(pair_index < frame_pairs + side_pairs, 1, 2)
    )
    anchor = jnp.where(
        which_axis == 0, 0, jnp.where(which_axis == 1, frame_pairs, frame_pairs + side_pairs)
    )
    pair_span = jnp.where(which_axis == 0, frame_pairs, side_pairs)
    frequency = jnp.exp(
        -math.log(10000.0)
        * (pair_index - anchor).astype(jnp.float32)
        / pair_span.astype(jnp.float32)
    )
    position = lattice.astype(jnp.float32)
    angles = jnp.zeros((lattice.shape[1], head_width), jnp.float32)
    for axis_number in range(3):
        chosen = jnp.where(which_axis == axis_number, frequency, 0.0)
        angles = angles + position[axis_number][:, None] * chosen[None, :]
    sign_flip = jnp.where(column < halfway, -1.0, 1.0).astype(jnp.float32)
    return (jnp.cos(angles), jnp.sin(angles) * sign_flip[None, :])


def partner(rows):
    return pltpu.roll(rows, rows.shape[1] // 2, 1)


def head_rotation(rows, cosine, sine):
    inverse = lax.rsqrt(jnp.mean(rows * rows, axis=1, keepdims=True) + 1e-06)
    normed = rows * inverse
    return normed, inverse, normed * cosine + partner(normed) * sine


def rotate_kernel(rows_ref, cosine_ref, sine_ref, out_ref):
    cosine, sine = cosine_ref[...], sine_ref[...]
    for start in range(0, rows_ref.shape[1], HEAD_SIZE):
        span = slice(start, start + HEAD_SIZE)
        rotated = head_rotation(rows_ref[:, span], cosine, sine)[2]
        out_ref[:, span] = rotated.astype(out_ref.dtype)


def rotate_heads(rows, cosine, sine):
    whole = pl.BlockSpec(memory_space=pltpu.VMEM)
    return pl.pallas_call(
        rotate_kernel,
        in_specs=[whole] * 3,
        out_specs=whole,
        out_shape=jax.ShapeDtypeStruct(rows.shape, jnp.bfloat16),
        compiler_params=pltpu.CompilerParams(vmem_limit_bytes=VMEM_BYTES),
        name="rotate_heads",
    )(rows, cosine, sine)


def drop(kernel, place, count=1):
    def run(*refs):
        kernel(*refs[:place], *refs[place + count :])

    return run


def turned_partner(turned):
    half = turned.shape[0] // 2
    return jnp.concatenate([turned[half:], turned[:half]], axis=0)


def attention_kernel(
    first, block, query_ref, key_ref, value_ref, cot_ref, cosine_ref, sine_ref, out_ref
):
    length, heads = query_ref.shape[0], out_ref.shape[0] // HEAD_SIZE
    scale = HEAD_SIZE ** (-0.5)
    for head in range(heads):
        span = slice((first + head) * HEAD_SIZE, (first + head + 1) * HEAD_SIZE)
        key, value = key_ref[:, span], value_ref[:, span]
        key_turned = key.T
        for start in range(0, length, block):
            rows = slice(start, start + block)
            cosine, sine = cosine_ref[:, rows], sine_ref[:, rows]
            query = query_ref[rows, span].T
            inverse = lax.rsqrt(jnp.mean(query * query, axis=0, keepdims=True) + 1e-06)
            normed = query * inverse
            rotated = normed * cosine + turned_partner(normed) * sine
            rotated = (rotated * (scale * math.log2(math.e))).astype(jnp.bfloat16)
            raised = jnp.exp2(jnp.dot(key, rotated, preferred_element_type=jnp.float32))
            grad = jnp.dot(value, cot_ref[rows, span].T, preferred_element_type=jnp.float32)
            product = raised * grad
            share = 1.0 / jnp.sum(raised, axis=0, keepdims=True)
            inner = jnp.sum(product, axis=0, keepdims=True) * share
            grad = (product - raised * inner).astype(jnp.bfloat16)
            grad = jnp.dot(key_turned, grad, preferred_element_type=jnp.float32) * (share * scale)
            grad = grad * cosine + turned_partner(grad * sine)
            shared = jnp.mean(grad * normed, axis=0, keepdims=True)
            grad = inverse * (grad - normed * shared)
            out_ref[head * HEAD_SIZE : (head + 1) * HEAD_SIZE, rows] = grad.astype(out_ref.dtype)


def attention_grad(query_pre, key, value, cot, cosine, sine, first, count, waits, block=512):
    length = query_pre.shape[0]
    whole = pl.BlockSpec(memory_space=pltpu.VMEM)
    return pl.pallas_call(
        drop(functools.partial(attention_kernel, first, block), 6, len(waits)),
        in_specs=[whole] * 6 + [pl.BlockSpec(memory_space=pl.ANY)] * len(waits),
        out_specs=whole,
        out_shape=jax.ShapeDtypeStruct((count * HEAD_SIZE, length), jnp.bfloat16),
        compiler_params=pltpu.CompilerParams(vmem_limit_bytes=VMEM_BYTES),
        name="attention_grad",
    )(query_pre, key, value, cot, cosine, sine, *waits)


def row_tile(rows):
    return 256 if rows % 256 == 0 else rows


def fisher_kernel(groups, first, *refs):
    rows, grads = refs[:groups], refs[groups:-4]
    own_ref, low_ref, held, done = refs[-4:]
    width, columns = low_ref.shape
    tile = row_tile(width)

    def squared(clip, grad, span):
        block = jnp.concatenate([ref[clip, :, span] for ref in rows], axis=0)
        grad = jnp.dot(grad, block, preferred_element_type=jnp.float32)
        return grad * grad

    copies = []
    for start in range(0, width, tile):
        span = slice(start, start + tile)
        total = jnp.zeros((columns, tile), jnp.float32)
        clip = 0
        for ref in grads:
            if len(ref.shape) == 2:
                total = total + squared(clip, ref[...], span)
                clip += 1
            else:
                total = lax.fori_loop(
                    0, ref.shape[0], lambda i, t, r=ref, s=span: t + squared(i, r[i], s), total
                )
                clip += ref.shape[0]
        fisher = total.T
        low_ref[span] = fisher.astype(low_ref.dtype)
        held[span] = fisher
        copies.append(
            pltpu.make_async_copy(
                held.at[span], own_ref.at[span, first : first + columns], done.at[len(copies)]
            )
        )
        copies[-1].start()
    for copy in copies:
        copy.wait()


def in_place(kernel, inputs, specs, previous, waits=()):
    extra = ([] if previous is None else [previous]) + list(waits)
    place = len(inputs)
    return (
        drop(kernel, place, len(extra)),
        list(inputs) + extra,
        list(specs) + [pl.BlockSpec(memory_space=pl.ANY)] * len(extra),
        {} if previous is None else {place: 0},
    )


def fisher_rows(rows, grads, first, total_columns, previous, waits):
    width = rows[0].shape[2]
    columns = grads[0].shape[-2]
    whole = pl.BlockSpec(memory_space=pltpu.VMEM)
    inputs = [*rows, *grads]
    kernel, inputs, specs, aliases = in_place(
        functools.partial(fisher_kernel, len(rows), first),
        inputs,
        [whole] * len(inputs),
        previous,
        waits,
    )
    return pl.pallas_call(
        kernel,
        in_specs=specs,
        out_specs=[pl.BlockSpec(memory_space=pl.ANY), whole],
        out_shape=[
            jax.ShapeDtypeStruct((width, total_columns), jnp.float32),
            jax.ShapeDtypeStruct((width, columns), jnp.bfloat16),
        ],
        scratch_shapes=[
            pltpu.VMEM((width, columns), jnp.float32),
            pltpu.SemaphoreType.DMA((width // row_tile(width),)),
        ],
        input_output_aliases=aliases,
        compiler_params=pltpu.CompilerParams(vmem_limit_bytes=FISHER_BYTES),
        name="fisher_rows",
    )(*inputs)


def merge_kernel(here_ref, there_ref, own_ref, other_ref, out_ref):
    zero = lax.axis_index("member") == 0
    here, there = to_f32(here_ref[...]) + damping, to_f32(there_ref[...]) + damping
    one, two = here * to_f32(own_ref[...]), there * to_f32(other_ref[...])
    upper = jnp.where(zero, one, two) + jnp.where(zero, two, one)
    out_ref[...] = upper / (here + there)


def merge_rows(here, there, own_weight, other_weight, first, offset, previous):
    width, columns = here.shape
    tile = width // 2
    plain = pl.BlockSpec((tile, columns), lambda i: (i, 0))
    part = pl.BlockSpec((pl.Element(tile), pl.Element(columns)), lambda i: (i * tile, first))
    other = pl.BlockSpec((pl.Element(tile), pl.Element(columns)), lambda i: (i * tile, offset))
    kernel, inputs, specs, aliases = in_place(
        merge_kernel, [here, there, own_weight, other_weight], [plain, plain, part, other], previous
    )
    return pl.pallas_call(
        kernel,
        grid=(width // tile,),
        in_specs=specs,
        out_specs=part,
        out_shape=jax.ShapeDtypeStruct(own_weight.shape, jnp.float32),
        input_output_aliases=aliases,
        compiler_params=pltpu.CompilerParams(vmem_limit_bytes=VMEM_BYTES),
        name="merge_rows",
    )(*inputs)


def spread_kernel(place_ref, rows_ref, *outs):
    rows = to_f32(rows_ref[...])
    average = jnp.mean(rows, axis=1, keepdims=True)
    centred = rows - average
    inverse = lax.rsqrt(jnp.mean(centred * centred, axis=1, keepdims=True) + 1e-06)
    size, width = len(outs), outs[0].shape[1]
    for away, out_ref in enumerate(outs):
        start = pl.multiple_of(lax.rem(place_ref[1] + away, size) * width, 128)
        part = to_f32(rows_ref[:, pl.ds(start, width)])
        out_ref[...] = ((part - average) * inverse).astype(out_ref.dtype)


def spread_rows(tokens, member, place, share, size):
    width = tokens.shape[1] // size
    return pl.pallas_call(
        spread_kernel,
        grid_spec=pltpu.PrefetchScalarGridSpec(
            num_scalar_prefetch=1,
            grid=(1,),
            in_specs=[pl.BlockSpec((share, tokens.shape[1]), lambda i, where: (where[0], 0))],
            out_specs=[pl.BlockSpec((share, width), lambda i, where: (0, 0))] * size,
        ),
        out_shape=[jax.ShapeDtypeStruct((share, width), jnp.bfloat16)] * size,
        compiler_params=pltpu.CompilerParams(vmem_limit_bytes=VMEM_BYTES),
        name="spread_rows",
    )(jnp.stack([member, place]).astype(jnp.int32), tokens)


def modulate(rows, modulation):
    return (rows * (1.0 + modulation[1:2]) + modulation[0:1]).astype(jnp.bfloat16)


def project_kernel(pieces, jobs, weights, waits, *refs):
    piece_refs, modulation_ref = refs[:pieces], refs[pieces]
    weight_refs = refs[pieces + 1 : pieces + 1 + weights]
    rows_ref, *outs = refs[pieces + 1 + weights + waits :]
    size = rows_ref.shape[0]
    share = piece_refs[0].shape[1]
    order = sorted(range(size), key=lambda away: -min(away, size - away))
    for away in order:
        modulation = modulation_ref[away]
        for i, ref in enumerate(piece_refs):
            rows_ref[away, i * share : (i + 1) * share] = modulate(to_f32(ref[away]), modulation)
        products = [
            jnp.dot(
                rows_ref[away, : count * share],
                weight_refs[index][...],
                preferred_element_type=jnp.float32,
            )
            for index, count in jobs
        ]
        products = products[0] if len(jobs) == 1 else jnp.concatenate(products, axis=0)
        if 2 * away == size:
            middle = products.shape[0] // 2
            outs[size][...] = products[middle:].astype(outs[size].dtype)
            products = products[:middle]
        outs[away][...] = products.astype(outs[away].dtype)


def project_rows(pieces, modulation, weights, jobs, waits):
    size, share, width = pieces[0].shape
    length = sum(count for _, count in jobs) * share
    columns = weights[0].shape[1]
    terms = [jax.ShapeDtypeStruct((length, columns), jnp.float32)] * size
    halves = [jax.ShapeDtypeStruct((length // 2, columns), jnp.bfloat16)] * 2
    terms = terms[: size // 2] + halves[:1] + terms[size // 2 + 1 :] + halves[1:]
    whole = pl.BlockSpec(memory_space=pltpu.VMEM)
    return pl.pallas_call(
        functools.partial(project_kernel, len(pieces), jobs, len(weights), len(waits)),
        in_specs=[whole] * (len(pieces) + 1 + len(weights))
        + [pl.BlockSpec(memory_space=pl.ANY)] * len(waits),
        out_specs=[whole] * (2 + size),
        out_shape=[jax.ShapeDtypeStruct((size, len(pieces) * share, width), jnp.bfloat16)] + terms,
        compiler_params=pltpu.CompilerParams(vmem_limit_bytes=VMEM_BYTES),
        name="project_rows",
    )(*pieces, modulation, *weights, *waits)


def to_f32(block):
    return block.astype(jnp.float32)


def behind(*arrays):
    return lax.optimization_barrier(arrays)


class Ring:
    def __init__(self, size):
        self.size = size
        self.place = lax.axis_index("seq")
        self.short = size <= 8 and size % 2 == 0

    def by_distance(self, blocks):
        return jnp.take(blocks, (self.place - jnp.arange(self.size)) % self.size, axis=0)

    def step(self, block, away):
        pairs = [(i, (i + away) % self.size) for i in range(self.size)]
        return lax.ppermute(block, "seq", pairs)

    def exchange(self, tokens, member, share):
        size = self.size
        width = tokens.shape[1] // size
        if self.short and width % 128 == 0:
            parts = spread_rows(tokens, member, self.place, share, size)
            return jnp.stack(
                list(parts[:1]) + [self.step(part, away) for away, part in enumerate(parts) if away]
            )
        mine = to_f32(lax.dynamic_slice_in_dim(tokens, member * share, share, 0))
        centred = mine - jnp.mean(mine, axis=1, keepdims=True)
        variance = jnp.mean(centred * centred, axis=1, keepdims=True)
        normed = (centred * lax.rsqrt(variance + 1e-06)).astype(jnp.bfloat16)
        parts = normed.reshape(share, size, width)
        return self.by_distance(
            lax.all_to_all(parts, "seq", split_axis=1, concat_axis=0, tiled=False)
        )

    def project(self, pieces, modulation, weights, jobs, waits):
        size, half = self.size, self.size // 2
        if not self.short:
            share = pieces[0].shape[1]
            rows = jax.vmap(modulate)(to_f32(jnp.concatenate(pieces, axis=1)), modulation)
            terms = [
                jnp.einsum(
                    "crw,wn->crn",
                    rows[:, : count * share],
                    weights[index],
                    preferred_element_type=jnp.float32,
                ).astype(jnp.bfloat16)
                for index, count in jobs
            ]
            return rows, jnp.concatenate(terms, axis=1), ()
        rows, *terms = project_rows(pieces, modulation, weights, jobs, waits)
        first = self.step(terms[half], 1), self.step(terms[size], -1)
        return rows, terms, first

    def sum(self, terms, first):
        size, half = self.size, self.size // 2
        if not self.short:
            return to_f32(lax.psum_scatter(self.by_distance(terms), "seq", tiled=False)), ()
        right, left = first
        middle = right.shape[0]
        for away in range(half - 1, 0, -1):
            term_right, term_left = terms[size - away], terms[away]
            if away == half - 1:
                term_right = jnp.concatenate(
                    [term_right[:middle] + to_f32(right), term_right[middle:]], axis=0
                )
                term_left = jnp.concatenate(
                    [term_left[:middle], term_left[middle:] + to_f32(left)], axis=0
                )
            else:
                term_right, term_left = term_right + to_f32(right), term_left + to_f32(left)
            right = self.step(term_right.astype(jnp.bfloat16), 1)
            left = self.step(term_left.astype(jnp.bfloat16), -1)
        if half == 1:
            return terms[0] + to_f32(jnp.concatenate([right, left], axis=0)), (right, left)
        return terms[0] + to_f32(right) + to_f32(left), (right, left)

    def gather(self, block):
        size, half = self.size, self.size // 2
        if not self.short:
            blocks = self.by_distance(lax.all_gather(block, "seq"))
            return [blocks], [blocks]
        blocks = [None] * size
        blocks[0] = block
        right, left = block, block
        for away in range(1, half):
            right, left = self.step(right, 1), self.step(left, -1)
            blocks[away], blocks[size - away] = right, left
        middle = block.shape[0] // 2
        blocks[half] = jnp.concatenate(
            [self.step(right[:middle], 1), self.step(left[middle:], -1)], axis=0
        )
        return blocks, [right, left]


def on_device(
    axes, tokens, lattice, timestep, time_weight, query_weight, key_weight, values, cotangent
):
    members, clips, heads = axes
    member = lax.axis_index("member")
    clip = lax.axis_index("seq")
    head = lax.axis_index("head")
    own_query = query_weight[0]
    width, columns = own_query.shape
    share = tokens.shape[0] // members

    ring = Ring(clips)

    def x_swap(block):
        return lax.ppermute(block, "member", [(i, i ^ 1) for i in range(members)])

    def h_swap(block, bits):
        return lax.ppermute(block, "head", [(i, i ^ bits) for i in range(heads)])

    own = ring.exchange(tokens, member, share)

    ordered = timestep[(clip - jnp.arange(clips)) % clips]
    features = time_features(ordered, time_weight.shape[1])
    modulation = jnp.einsum(
        "cf,jfd->cjd", features, time_weight, preferred_element_type=jnp.float32
    )

    def both(block):
        return [block, h_swap(block, 1)]

    weights = [own_query, key_weight]
    jobs = [(0, 2), (1, 2)]
    near_y, near_x = h_swap(own, 2), x_swap(own)
    rows_own, terms_own, first_own = ring.project(both(own), modulation, weights, jobs, [])
    near_y, _ = behind(near_y, rows_own)
    far = x_swap(near_y)
    sums_own, last_own = ring.sum(terms_own, first_own)
    near_y = behind(near_y, *first_own)[0]
    rows_y, terms_y, first_y = ring.project(both(near_y), modulation, weights, jobs, [rows_own])
    sums_y, _ = ring.sum(terms_y, first_y)
    rows_x, terms_x, first_x = ring.project(
        both(near_x) + both(far), modulation, [own_query], [(0, 4)], [rows_y, *first_y, *last_own]
    )
    lines = 2 * share
    key_here = jnp.concatenate([sums_own[lines:], sums_y[lines:]], axis=0)

    grid = lattice.reshape(3, 2, 2, members, share).transpose(0, 3, 1, 2, 4)
    for axis, bit in ((1, member), (2, head // 2), (3, head % 2)):
        grid = jnp.where(bit == 1, jnp.flip(grid, axis), grid)
    cosine, sine = rope_tables(grid.reshape(3, -1), HEAD_SIZE)

    pair = jnp.stack([values, cotangent[0]])
    blocks = []
    for bits in range(heads):
        block = lax.dynamic_slice_in_dim(pair, (head ^ bits) * columns, columns, 2)
        blocks.append(h_swap(block, bits) if bits else block)
    halves = jnp.stack(blocks, axis=1).reshape(2, heads, members, share, columns)
    halves = jnp.concatenate(
        [lax.dynamic_slice_in_dim(halves, member ^ i, 1, 2)[:, :, 0] for i in range(members)], axis=1
    ).reshape(2, members * heads * share, columns)
    value_rows, cot_rows = halves[0], halves[1]

    head_count = columns // HEAD_SIZE
    last_heads = max(1, head_count // 5)
    bounds = [0, (head_count - last_heads) // 2, head_count - last_heads, head_count]
    cut = bounds[1] * HEAD_SIZE
    early, _ = behind(own_query[:, :cut], far)
    early = x_swap(early)

    rows_here = key_here.shape[0]
    key_here = rotate_heads(key_here, cosine[:rows_here], sine[:rows_here])
    key_here, early = behind(key_here, early, *first_x)[:2]
    key_there = x_swap(key_here)
    key_rows = jnp.concatenate([key_here, key_there], axis=0)
    late, _ = behind(own_query[:, cut:], key_there)
    late = x_swap(late)

    query_x, _ = ring.sum(terms_x, first_x)
    query_pre = jnp.concatenate([sums_own[:lines], sums_y[:lines], query_x], axis=0)
    operands = query_pre, key_rows, value_rows, cot_rows, cosine.T, sine.T
    spans = [(first, last) for first, last in zip(bounds[:-1], bounds[1:]) if first < last]
    grads, gathered, waits = [], [], []
    for i, (first, last) in enumerate(spans):
        grads.append(attention_grad(*operands, first, last - first, waits + [late] * (i == 1)))
        blocks, waits = ring.gather(grads[-1])
        gathered.append(blocks)
    fisher, merged = None, None
    for i, (first, _) in enumerate(spans):
        first = first * HEAD_SIZE
        rows = [rows_own, rows_y, rows_x]
        fisher, low = fisher_rows(rows, gathered[i], first, columns, fisher, grads[i + 2 : i + 3])
        other, offset = (late, first - cut) if first >= cut else (early, first)
        merged = merge_rows(low, x_swap(low), own_query, other, first, offset, merged)
    return fisher[None], merged


def solution(mesh):
    axes = (mesh.shape["member"], mesh.shape["seq"], mesh.shape["head"])
    return jax.shard_map(
        functools.partial(on_device, axes),
        mesh=mesh,
        in_specs=(
            P(("seq", "head"), None),
            P(None, "seq"),
            P(),
            P(None, None, "seq"),
            P("member", "seq", "head"),
            P("seq", "head"),
            P(("seq", "head"), None),
            P("member", ("seq", "head"), None),
        ),
        out_specs=(P("member", "seq", "head"), P("seq", "head")),
        check_vma=False,
    )
```

```python
import functools
import math

import jax
import jax.numpy as jnp
from jax import lax
from jax.experimental import pallas as pl
from jax.experimental.pallas import tpu as pltpu
from jax.sharding import PartitionSpec as P

HEAD_SIZE = 128
damping = 0.01
VMEM_BYTES = 24 * 1024 * 1024
FISHER_BYTES = 32 * 1024 * 1024


def time_features(timestep, feature_count):
    halfway = feature_count // 2
    ladder = jnp.arange(halfway).astype(jnp.float32)
    frequency = jnp.exp(-math.log(10000.0) * 2.0 * ladder / feature_count)
    angles = timestep.astype(jnp.float32)[:, None] * frequency[None, :]
    return jnp.concatenate([jnp.cos(angles), jnp.sin(angles)], axis=1).astype(jnp.bfloat16)


def rope_tables(lattice, head_width):
    halfway = head_width // 2
    side_pairs = head_width // 6
    frame_pairs = halfway - 2 * side_pairs
    column = jnp.arange(head_width)
    pair_index = column % halfway
    which_axis = jnp.where(
        pair_index < frame_pairs, 0, jnp.where(pair_index < frame_pairs + side_pairs, 1, 2)
    )
    anchor = jnp.where(
        which_axis == 0, 0, jnp.where(which_axis == 1, frame_pairs, frame_pairs + side_pairs)
    )
    pair_span = jnp.where(which_axis == 0, frame_pairs, side_pairs)
    frequency = jnp.exp(
        -math.log(10000.0)
        * (pair_index - anchor).astype(jnp.float32)
        / pair_span.astype(jnp.float32)
    )
    position = lattice.astype(jnp.float32)
    angles = jnp.zeros((lattice.shape[1], head_width), jnp.float32)
    for axis_number in range(3):
        chosen = jnp.where(which_axis == axis_number, frequency, 0.0)
        angles = angles + position[axis_number][:, None] * chosen[None, :]
    sign_flip = jnp.where(column < halfway, -1.0, 1.0).astype(jnp.float32)
    return (jnp.cos(angles), jnp.sin(angles) * sign_flip[None, :])


def partner(rows):
    return pltpu.roll(rows, rows.shape[1] // 2, 1)


def head_rotation(rows, cosine, sine):
    inverse = lax.rsqrt(jnp.mean(rows * rows, axis=1, keepdims=True) + 1e-06)
    normed = rows * inverse
    return normed, inverse, normed * cosine + partner(normed) * sine


def rotate_kernel(rows_ref, cosine_ref, sine_ref, out_ref):
    cosine, sine = cosine_ref[...], sine_ref[...]
    for start in range(0, rows_ref.shape[1], HEAD_SIZE):
        span = slice(start, start + HEAD_SIZE)
        rotated = head_rotation(rows_ref[:, span], cosine, sine)[2]
        out_ref[:, span] = rotated.astype(out_ref.dtype)


def rotate_heads(rows, cosine, sine):
    whole = pl.BlockSpec(memory_space=pltpu.VMEM)
    return pl.pallas_call(
        rotate_kernel,
        in_specs=[whole] * 3,
        out_specs=whole,
        out_shape=jax.ShapeDtypeStruct(rows.shape, jnp.bfloat16),
        compiler_params=pltpu.CompilerParams(vmem_limit_bytes=VMEM_BYTES),
        name="rotate_heads",
    )(rows, cosine, sine)


def drop(kernel, place, count=1):
    def run(*refs):
        kernel(*refs[:place], *refs[place + count :])

    return run


def turned_partner(turned):
    half = turned.shape[0] // 2
    return jnp.concatenate([turned[half:], turned[:half]], axis=0)


def attention_kernel(
    own_first, first, block, query_ref, key_ref, value_ref, cot_ref, cosine_ref, sine_ref, out_ref
):
    length, heads = query_ref.shape[0], out_ref.shape[0] // HEAD_SIZE
    scale = HEAD_SIZE ** (-0.5)
    for head in range(heads):
        span = slice((first + head) * HEAD_SIZE, (first + head + 1) * HEAD_SIZE)
        own = slice((own_first + head) * HEAD_SIZE, (own_first + head + 1) * HEAD_SIZE)
        key, value = key_ref[:, span], value_ref[:, span]
        key_turned = key.T
        for start in range(0, length, block):
            rows = slice(start, start + block)
            cosine, sine = cosine_ref[:, rows], sine_ref[:, rows]
            query = query_ref[rows, own].T
            inverse = lax.rsqrt(jnp.mean(query * query, axis=0, keepdims=True) + 1e-06)
            normed = query * inverse
            rotated = normed * cosine + turned_partner(normed) * sine
            rotated = (rotated * (scale * math.log2(math.e))).astype(jnp.bfloat16)
            raised = jnp.exp2(jnp.dot(key, rotated, preferred_element_type=jnp.float32))
            grad = jnp.dot(value, cot_ref[rows, span].T, preferred_element_type=jnp.float32)
            product = raised * grad
            share = 1.0 / jnp.sum(raised, axis=0, keepdims=True)
            inner = jnp.sum(product, axis=0, keepdims=True) * share
            grad = (product - raised * inner).astype(jnp.bfloat16)
            grad = jnp.dot(key_turned, grad, preferred_element_type=jnp.float32) * (share * scale)
            grad = grad * cosine + turned_partner(grad * sine)
            shared = jnp.mean(grad * normed, axis=0, keepdims=True)
            grad = inverse * (grad - normed * shared)
            out_ref[head * HEAD_SIZE : (head + 1) * HEAD_SIZE, rows] = grad.astype(out_ref.dtype)


def attention_grad(
    query_pre, key, value, cot, cosine, sine, own_first, first, count, waits, block=512
):
    length = query_pre.shape[0]
    whole = pl.BlockSpec(memory_space=pltpu.VMEM)
    return pl.pallas_call(
        drop(functools.partial(attention_kernel, own_first, first, block), 6, len(waits)),
        in_specs=[whole] * 6 + [pl.BlockSpec(memory_space=pl.ANY)] * len(waits),
        out_specs=whole,
        out_shape=jax.ShapeDtypeStruct((count * HEAD_SIZE, length), jnp.bfloat16),
        compiler_params=pltpu.CompilerParams(vmem_limit_bytes=VMEM_BYTES),
        name="attention_grad",
    )(query_pre, key, value, cot, cosine, sine, *waits)


def row_tile(rows):
    return 256 if rows % 256 == 0 else rows


def fisher_kernel(groups, first, *refs):
    rows, grads = refs[:groups], refs[groups:-4]
    own_ref, low_ref, held, done = refs[-4:]
    width, columns = low_ref.shape
    tile = row_tile(width)

    def squared(clip, grad, span):
        block = jnp.concatenate([ref[clip, :, span] for ref in rows], axis=0)
        grad = jnp.dot(grad, block, preferred_element_type=jnp.float32)
        return grad * grad

    copies = []
    for start in range(0, width, tile):
        span = slice(start, start + tile)
        total = jnp.zeros((columns, tile), jnp.float32)
        clip = 0
        for ref in grads:
            if len(ref.shape) == 2:
                total = total + squared(clip, ref[...], span)
                clip += 1
            else:
                total = lax.fori_loop(
                    0, ref.shape[0], lambda i, t, r=ref, s=span: t + squared(i, r[i], s), total
                )
                clip += ref.shape[0]
        fisher = total.T
        low_ref[span] = fisher.astype(low_ref.dtype)
        held[span] = fisher
        copies.append(
            pltpu.make_async_copy(
                held.at[span], own_ref.at[span, first : first + columns], done.at[len(copies)]
            )
        )
        copies[-1].start()
    for copy in copies:
        copy.wait()


def in_place(kernel, inputs, specs, previous, waits=()):
    extra = ([] if previous is None else [previous]) + list(waits)
    place = len(inputs)
    return (
        drop(kernel, place, len(extra)),
        list(inputs) + extra,
        list(specs) + [pl.BlockSpec(memory_space=pl.ANY)] * len(extra),
        {} if previous is None else {place: 0},
    )


def fisher_rows(rows, grads, first, total_columns, previous, waits):
    width = rows[0].shape[2]
    columns = grads[0].shape[-2]
    whole = pl.BlockSpec(memory_space=pltpu.VMEM)
    inputs = [*rows, *grads]
    kernel, inputs, specs, aliases = in_place(
        functools.partial(fisher_kernel, len(rows), first),
        inputs,
        [whole] * len(inputs),
        previous,
        waits,
    )
    return pl.pallas_call(
        kernel,
        in_specs=specs,
        out_specs=[pl.BlockSpec(memory_space=pl.ANY), whole],
        out_shape=[
            jax.ShapeDtypeStruct((width, total_columns), jnp.float32),
            jax.ShapeDtypeStruct((width, columns), jnp.bfloat16),
        ],
        scratch_shapes=[
            pltpu.VMEM((width, columns), jnp.float32),
            pltpu.SemaphoreType.DMA((width // row_tile(width),)),
        ],
        input_output_aliases=aliases,
        compiler_params=pltpu.CompilerParams(vmem_limit_bytes=FISHER_BYTES),
        name="fisher_rows",
    )(*inputs)


def merge_kernel(here_ref, there_ref, own_ref, other_ref, out_ref):
    zero = lax.axis_index("member") == 0
    here, there = to_f32(here_ref[...]) + damping, to_f32(there_ref[...]) + damping
    one, two = here * to_f32(own_ref[...]), there * to_f32(other_ref[...])
    upper = jnp.where(zero, one, two) + jnp.where(zero, two, one)
    out_ref[...] = upper / (here + there)


def merge_rows(here, there, own_weight, other_weight, first, offset, previous):
    width, columns = here.shape
    tile = width // 2
    plain = pl.BlockSpec((tile, columns), lambda i: (i, 0))
    part = pl.BlockSpec((pl.Element(tile), pl.Element(columns)), lambda i: (i * tile, first))
    other = pl.BlockSpec((pl.Element(tile), pl.Element(columns)), lambda i: (i * tile, offset))
    kernel, inputs, specs, aliases = in_place(
        merge_kernel, [here, there, own_weight, other_weight], [plain, plain, part, other], previous
    )
    return pl.pallas_call(
        kernel,
        grid=(width // tile,),
        in_specs=specs,
        out_specs=part,
        out_shape=jax.ShapeDtypeStruct(own_weight.shape, jnp.float32),
        input_output_aliases=aliases,
        compiler_params=pltpu.CompilerParams(vmem_limit_bytes=VMEM_BYTES),
        name="merge_rows",
    )(*inputs)


def spread_kernel(place_ref, rows_ref, *outs):
    rows = to_f32(rows_ref[...])
    average = jnp.mean(rows, axis=1, keepdims=True)
    centred = rows - average
    inverse = lax.rsqrt(jnp.mean(centred * centred, axis=1, keepdims=True) + 1e-06)
    size, width = len(outs), outs[0].shape[1]
    for away, out_ref in enumerate(outs):
        start = pl.multiple_of(lax.rem(place_ref[1] + away, size) * width, 128)
        part = to_f32(rows_ref[:, pl.ds(start, width)])
        out_ref[...] = ((part - average) * inverse).astype(out_ref.dtype)


def spread_rows(tokens, member, place, share, size):
    width = tokens.shape[1] // size
    return pl.pallas_call(
        spread_kernel,
        grid_spec=pltpu.PrefetchScalarGridSpec(
            num_scalar_prefetch=1,
            grid=(1,),
            in_specs=[pl.BlockSpec((share, tokens.shape[1]), lambda i, where: (where[0], 0))],
            out_specs=[pl.BlockSpec((share, width), lambda i, where: (0, 0))] * size,
        ),
        out_shape=[jax.ShapeDtypeStruct((share, width), jnp.bfloat16)] * size,
        compiler_params=pltpu.CompilerParams(vmem_limit_bytes=VMEM_BYTES),
        name="spread_rows",
    )(jnp.stack([member, place]).astype(jnp.int32), tokens)


def modulate(rows, modulation):
    return (rows * (1.0 + modulation[1:2]) + modulation[0:1]).astype(jnp.bfloat16)


def project_kernel(pieces, jobs, cuts, weights, waits, *refs):
    piece_refs, modulation_ref = refs[:pieces], refs[pieces]
    weight_refs = refs[pieces + 1 : pieces + 1 + weights]
    rows_ref, *outs = refs[pieces + 1 + weights + waits :]
    size = rows_ref.shape[0]
    share = piece_refs[0].shape[1]
    order = sorted(range(size), key=lambda away: -min(away, size - away))
    for away in order:
        modulation = modulation_ref[away]
        for i, ref in enumerate(piece_refs):
            rows_ref[away, i * share : (i + 1) * share] = modulate(to_f32(ref[away]), modulation)
        products = [
            jnp.dot(
                rows_ref[away, : count * share],
                weight_refs[index][...],
                preferred_element_type=jnp.float32,
            )
            for index, count in jobs
        ]
        products = products[0] if len(jobs) == 1 else jnp.concatenate(products, axis=0)
        products = products.astype(outs[0].dtype)
        middle = products.shape[0] // 2
        for part, (start, stop) in enumerate(zip(cuts[:-1], cuts[1:])):
            part_outs = outs[part * (size + 1) : (part + 1) * (size + 1)]
            if 2 * away == size:
                part_outs[away][...] = products[:middle, start:stop]
                part_outs[size][...] = products[middle:, start:stop]
            else:
                part_outs[away][...] = products[:, start:stop]


def project_rows(pieces, modulation, weights, jobs, cuts, waits):
    size, share, width = pieces[0].shape
    length = sum(count for _, count in jobs) * share
    lengths = [length // 2 if 2 * away == size else length for away in range(size)] + [length // 2]
    terms = [
        jax.ShapeDtypeStruct((lines, stop - start), jnp.bfloat16)
        for start, stop in zip(cuts[:-1], cuts[1:])
        for lines in lengths
    ]
    whole = pl.BlockSpec(memory_space=pltpu.VMEM)
    return pl.pallas_call(
        functools.partial(project_kernel, len(pieces), jobs, cuts, len(weights), len(waits)),
        in_specs=[whole] * (len(pieces) + 1 + len(weights))
        + [pl.BlockSpec(memory_space=pl.ANY)] * len(waits),
        out_specs=[pl.BlockSpec()] * (1 + len(terms)),
        out_shape=[jax.ShapeDtypeStruct((size, len(pieces) * share, width), jnp.bfloat16)] + terms,
        compiler_params=pltpu.CompilerParams(vmem_limit_bytes=VMEM_BYTES),
        name="project_rows",
    )(*pieces, modulation, *weights, *waits)


def to_f32(block):
    return block.astype(jnp.float32)


def added(term, message):
    return (to_f32(term) + to_f32(message)).astype(term.dtype)


def behind(*arrays):
    return lax.optimization_barrier(arrays)


class Ring:
    def __init__(self, size):
        self.size = size
        self.place = lax.axis_index("seq")
        self.short = size <= 8 and size % 2 == 0

    def by_distance(self, blocks):
        return jnp.take(blocks, (self.place - jnp.arange(self.size)) % self.size, axis=0)

    def step(self, block, away):
        pairs = [(i, (i + away) % self.size) for i in range(self.size)]
        return lax.ppermute(block, "seq", pairs)

    def exchange(self, tokens, member, share):
        size = self.size
        width = tokens.shape[1] // size
        if self.short and width % 128 == 0:
            parts = spread_rows(tokens, member, self.place, share, size)
            return jnp.stack(
                list(parts[:1]) + [self.step(part, away) for away, part in enumerate(parts) if away]
            )
        mine = to_f32(lax.dynamic_slice_in_dim(tokens, member * share, share, 0))
        centred = mine - jnp.mean(mine, axis=1, keepdims=True)
        variance = jnp.mean(centred * centred, axis=1, keepdims=True)
        normed = (centred * lax.rsqrt(variance + 1e-06)).astype(jnp.bfloat16)
        parts = normed.reshape(share, size, width)
        return self.by_distance(
            lax.all_to_all(parts, "seq", split_axis=1, concat_axis=0, tiled=False)
        )

    def project(self, pieces, modulation, weights, jobs, cuts, waits):
        size, half = self.size, self.size // 2
        if not self.short:
            share = pieces[0].shape[1]
            rows = jax.vmap(modulate)(to_f32(jnp.concatenate(pieces, axis=1)), modulation)
            terms = [
                jnp.einsum(
                    "crw,wn->crn",
                    rows[:, : count * share],
                    weights[index],
                    preferred_element_type=jnp.float32,
                ).astype(jnp.bfloat16)
                for index, count in jobs
            ]
            terms = jnp.concatenate(terms, axis=1)
            return rows, [(terms[:, :, a:b], ()) for a, b in zip(cuts[:-1], cuts[1:])]
        rows, *terms = project_rows(pieces, modulation, weights, jobs, cuts, waits)
        parts = []
        for part in range(len(cuts) - 1):
            own = terms[part * (size + 1) : (part + 1) * (size + 1)]
            parts.append((own, (self.step(own[half], 1), self.step(own[size], -1))))
        return rows, parts

    def sum(self, terms, first):
        size, half = self.size, self.size // 2
        if not self.short:
            return to_f32(lax.psum_scatter(self.by_distance(terms), "seq", tiled=False)), ()
        right, left = first
        middle = right.shape[0]
        for away in range(half - 1, 0, -1):
            term_right, term_left = terms[size - away], terms[away]
            if away == half - 1:
                term_right = jnp.concatenate(
                    [added(term_right[:middle], right), term_right[middle:]], axis=0
                )
                term_left = jnp.concatenate(
                    [term_left[:middle], added(term_left[middle:], left)], axis=0
                )
            else:
                term_right, term_left = added(term_right, right), added(term_left, left)
            right, left = self.step(term_right, 1), self.step(term_left, -1)
        if half == 1:
            return to_f32(terms[0]) + to_f32(jnp.concatenate([right, left], axis=0)), (right, left)
        return to_f32(terms[0]) + to_f32(right) + to_f32(left), (right, left)

    def spread(self, block):
        size, half = self.size, self.size // 2
        if not self.short:
            return [self.by_distance(lax.all_gather(block, "seq"))]
        blocks = [None] * size
        blocks[0] = block
        for away in range(1, half):
            blocks[away] = self.step(blocks[away - 1], 1)
            blocks[-away] = self.step(blocks[1 - away], -1)
        return blocks

    def complete(self, blocks, after):
        half = self.size // 2
        if not self.short:
            return blocks, blocks
        right, left = blocks[half - 1], blocks[(half + 1) % self.size]
        right, left = behind(right, left, *after)[:2]
        middle = right.shape[0] // 2
        last = [self.step(right[:middle], 1), self.step(left[middle:], -1)]
        return blocks[:half] + [jnp.concatenate(last, axis=0)] + blocks[half + 1 :], last


def on_device(
    axes, tokens, lattice, timestep, time_weight, query_weight, key_weight, values, cotangent
):
    members, clips, heads = axes
    member = lax.axis_index("member")
    clip = lax.axis_index("seq")
    head = lax.axis_index("head")
    own_query = query_weight[0]
    width, columns = own_query.shape
    share = tokens.shape[0] // members

    ring = Ring(clips)

    def x_swap(block):
        return lax.ppermute(block, "member", [(i, i ^ 1) for i in range(members)])

    def h_swap(block, bits):
        return lax.ppermute(block, "head", [(i, i ^ bits) for i in range(heads)])

    own = ring.exchange(tokens, member, share)

    ordered = timestep[(clip - jnp.arange(clips)) % clips]
    features = time_features(ordered, time_weight.shape[1])
    modulation = jnp.einsum(
        "cf,jfd->cjd", features, time_weight, preferred_element_type=jnp.float32
    )

    def both(block):
        return [block, h_swap(block, 1)]

    weights = [own_query, key_weight]
    head_count = columns // HEAD_SIZE
    last_heads = max(1, head_count // 5)
    bounds = [0, (head_count - last_heads) // 2, head_count - last_heads, head_count]
    cut = bounds[1] * HEAD_SIZE
    jobs, full = [(0, 2), (1, 2)], [0, columns]
    near_y, near_x = h_swap(own, 2), x_swap(own)
    rows_own, [(terms, first_own)] = ring.project(both(own), modulation, weights, jobs, full, [])
    sums_own, _ = ring.sum(terms, first_own)
    near_y, _ = behind(near_y, rows_own)
    far = x_swap(near_y)
    near_y = behind(near_y, *first_own)[0]
    rows_y, [(terms_y, first_y)] = ring.project(
        both(near_y), modulation, weights, jobs, full, [rows_own]
    )
    rows_x, parts_x = ring.project(
        both(near_x) + both(far),
        modulation,
        [own_query],
        [(0, 4)],
        [0, cut, columns] if cut else full,
        [rows_y],
    )
    sums_y, _ = ring.sum(terms_y, behind(*first_y, rows_x)[:-1])
    lines = 2 * share
    key_here = jnp.concatenate([sums_own[lines:], sums_y[lines:]], axis=0)

    grid = lattice.reshape(3, 2, 2, members, share).transpose(0, 3, 1, 2, 4)
    for axis, bit in ((1, member), (2, head // 2), (3, head % 2)):
        grid = jnp.where(bit == 1, jnp.flip(grid, axis), grid)
    cosine, sine = rope_tables(grid.reshape(3, -1), HEAD_SIZE)

    pair = jnp.stack([values, cotangent[0]])
    blocks = []
    for bits in range(heads):
        block = lax.dynamic_slice_in_dim(pair, (head ^ bits) * columns, columns, 2)
        blocks.append(h_swap(block, bits) if bits else block)
    halves = jnp.stack(blocks, axis=1).reshape(2, heads, members, share, columns)
    halves = jnp.concatenate(
        [lax.dynamic_slice_in_dim(halves, member ^ i, 1, 2)[:, :, 0] for i in range(members)], axis=1
    ).reshape(2, members * heads * share, columns)
    value_rows, cot_rows = halves[0], halves[1]

    early, _ = behind(own_query[:, :cut], far)
    early = x_swap(early)

    rows_here = key_here.shape[0]
    key_here = rotate_heads(key_here, cosine[:rows_here], sine[:rows_here])
    key_here, early = behind(key_here, early, *parts_x[0][1])[:2]
    key_there = x_swap(key_here)
    key_rows = jnp.concatenate([key_here, key_there], axis=0)
    late, _ = behind(own_query[:, cut:], key_there)
    late = x_swap(late)

    queries, start = [], 0
    for terms, first in parts_x:
        query_x, _ = ring.sum(terms, first)
        span = slice(start, start + query_x.shape[1])
        queries.append(
            jnp.concatenate([sums_own[:lines, span], sums_y[:lines, span], query_x], axis=0)
        )
        start = span.stop

    operands = key_rows, value_rows, cot_rows, cosine.T, sine.T
    spans = [(first, last) for first, last in zip(bounds[:-1], bounds[1:]) if first < last]
    fisher, merged, lows, waits, ready = None, None, [], [], []
    for i, (first, last) in enumerate(spans):
        part = 1 if len(queries) > 1 and first * HEAD_SIZE >= cut else 0
        grad_query = attention_grad(
            queries[part], *operands, first - part * bounds[1], first, last - first, ready
        )
        blocks = ring.spread(behind(grad_query, *waits)[0] if i else grad_query)
        waits = [block for block in blocks[1:] if block is not None]
        ready = [grad_query] if i else [grad_query, *waits]
        blocks, far_blocks = ring.complete(blocks, lows[-1:])
        if i == 0:
            waits = [*far_blocks, late]
        first = first * HEAD_SIZE
        fisher, low = fisher_rows([rows_own, rows_y, rows_x], blocks, first, columns, fisher, [])
        lows.append(low)
        other, offset = (late, first - cut) if first >= cut else (early, first)
        merged = merge_rows(low, x_swap(low), own_query, other, first, offset, merged)
    return fisher[None], merged


def solution(mesh):
    axes = (mesh.shape["member"], mesh.shape["seq"], mesh.shape["head"])
    return jax.shard_map(
        functools.partial(on_device, axes),
        mesh=mesh,
        in_specs=(
            P(("seq", "head"), None),
            P(None, "seq"),
            P(),
            P(None, None, "seq"),
            P("member", "seq", "head"),
            P("seq", "head"),
            P(("seq", "head"), None),
            P("member", ("seq", "head"), None),
        ),
        out_specs=(P("member", "seq", "head"), P("seq", "head")),
        check_vma=False,
    )
```

```python
import functools
import math

import jax
import jax.numpy as jnp
from jax import lax
from jax.experimental import pallas as pl
from jax.experimental.pallas import tpu as pltpu
from jax.sharding import PartitionSpec as P

HEAD_SIZE = 128
damping = 0.01
VMEM_BYTES = 24 * 1024 * 1024
FISHER_BYTES = 32 * 1024 * 1024


def time_features(timestep, feature_count):
    halfway = feature_count // 2
    ladder = jnp.arange(halfway).astype(jnp.float32)
    frequency = jnp.exp(-math.log(10000.0) * 2.0 * ladder / feature_count)
    angles = timestep.astype(jnp.float32)[:, None] * frequency[None, :]
    return jnp.concatenate([jnp.cos(angles), jnp.sin(angles)], axis=1).astype(jnp.bfloat16)


def rope_tables(lattice, head_width):
    halfway = head_width // 2
    side_pairs = head_width // 6
    frame_pairs = halfway - 2 * side_pairs
    column = jnp.arange(head_width)
    pair_index = column % halfway
    which_axis = jnp.where(
        pair_index < frame_pairs, 0, jnp.where(pair_index < frame_pairs + side_pairs, 1, 2)
    )
    anchor = jnp.where(
        which_axis == 0, 0, jnp.where(which_axis == 1, frame_pairs, frame_pairs + side_pairs)
    )
    pair_span = jnp.where(which_axis == 0, frame_pairs, side_pairs)
    frequency = jnp.exp(
        -math.log(10000.0)
        * (pair_index - anchor).astype(jnp.float32)
        / pair_span.astype(jnp.float32)
    )
    position = lattice.astype(jnp.float32)
    angles = jnp.zeros((lattice.shape[1], head_width), jnp.float32)
    for axis_number in range(3):
        chosen = jnp.where(which_axis == axis_number, frequency, 0.0)
        angles = angles + position[axis_number][:, None] * chosen[None, :]
    sign_flip = jnp.where(column < halfway, -1.0, 1.0).astype(jnp.float32)
    return (jnp.cos(angles), jnp.sin(angles) * sign_flip[None, :])


def partner(rows):
    return pltpu.roll(rows, rows.shape[1] // 2, 1)


def head_rotation(rows, cosine, sine):
    inverse = lax.rsqrt(jnp.mean(rows * rows, axis=1, keepdims=True) + 1e-06)
    normed = rows * inverse
    return normed, inverse, normed * cosine + partner(normed) * sine


def rotate_kernel(rows_ref, cosine_ref, sine_ref, out_ref):
    cosine, sine = cosine_ref[...], sine_ref[...]
    for start in range(0, rows_ref.shape[1], HEAD_SIZE):
        span = slice(start, start + HEAD_SIZE)
        rotated = head_rotation(rows_ref[:, span], cosine, sine)[2]
        out_ref[:, span] = rotated.astype(out_ref.dtype)


def rotate_heads(rows, cosine, sine):
    whole = pl.BlockSpec(memory_space=pltpu.VMEM)
    return pl.pallas_call(
        rotate_kernel,
        in_specs=[whole] * 3,
        out_specs=whole,
        out_shape=jax.ShapeDtypeStruct(rows.shape, jnp.bfloat16),
        compiler_params=pltpu.CompilerParams(vmem_limit_bytes=VMEM_BYTES),
        name="rotate_heads",
    )(rows, cosine, sine)


def drop(kernel, place, count=1):
    def run(*refs):
        kernel(*refs[:place], *refs[place + count :])

    return run


def turned_partner(turned):
    half = turned.shape[0] // 2
    return jnp.concatenate([turned[half:], turned[:half]], axis=0)


def attention_kernel(
    own_first, first, block, query_ref, key_ref, value_ref, cot_ref, cosine_ref, sine_ref, out_ref
):
    length, heads = query_ref.shape[0], out_ref.shape[0] // HEAD_SIZE
    scale = HEAD_SIZE ** (-0.5)
    for head in range(heads):
        span = slice((first + head) * HEAD_SIZE, (first + head + 1) * HEAD_SIZE)
        own = slice((own_first + head) * HEAD_SIZE, (own_first + head + 1) * HEAD_SIZE)
        key, value = key_ref[:, span], value_ref[:, span]
        key_turned = key.T
        for start in range(0, length, block):
            rows = slice(start, start + block)
            cosine, sine = cosine_ref[:, rows], sine_ref[:, rows]
            query = query_ref[rows, own].T
            inverse = lax.rsqrt(jnp.mean(query * query, axis=0, keepdims=True) + 1e-06)
            normed = query * inverse
            rotated = normed * cosine + turned_partner(normed) * sine
            rotated = (rotated * (scale * math.log2(math.e))).astype(jnp.bfloat16)
            raised = jnp.exp2(jnp.dot(key, rotated, preferred_element_type=jnp.float32))
            grad = jnp.dot(value, cot_ref[rows, span].T, preferred_element_type=jnp.float32)
            product = raised * grad
            share = 1.0 / jnp.sum(raised, axis=0, keepdims=True)
            inner = jnp.sum(product, axis=0, keepdims=True) * share
            grad = (product - raised * inner).astype(jnp.bfloat16)
            grad = jnp.dot(key_turned, grad, preferred_element_type=jnp.float32) * (share * scale)
            grad = grad * cosine + turned_partner(grad * sine)
            shared = jnp.mean(grad * normed, axis=0, keepdims=True)
            grad = inverse * (grad - normed * shared)
            out_ref[head * HEAD_SIZE : (head + 1) * HEAD_SIZE, rows] = grad.astype(out_ref.dtype)


def attention_grad(
    query_pre, key, value, cot, cosine, sine, own_first, first, count, waits, block=512
):
    length = query_pre.shape[0]
    whole = pl.BlockSpec(memory_space=pltpu.VMEM)
    return pl.pallas_call(
        drop(functools.partial(attention_kernel, own_first, first, block), 6, len(waits)),
        in_specs=[whole] * 6 + [pl.BlockSpec(memory_space=pl.ANY)] * len(waits),
        out_specs=whole,
        out_shape=jax.ShapeDtypeStruct((count * HEAD_SIZE, length), jnp.bfloat16),
        compiler_params=pltpu.CompilerParams(vmem_limit_bytes=VMEM_BYTES),
        name="attention_grad",
    )(query_pre, key, value, cot, cosine, sine, *waits)


def row_tile(rows):
    return 256 if rows % 256 == 0 else rows


def fisher_kernel(groups, first, *refs):
    rows, grads = refs[:groups], refs[groups:-4]
    own_ref, low_ref, held, done = refs[-4:]
    width, columns = low_ref.shape
    tile = row_tile(width)

    def squared(clip, grad, span):
        block = jnp.concatenate([ref[clip, :, span] for ref in rows], axis=0)
        grad = jnp.dot(grad, block, preferred_element_type=jnp.float32)
        return grad * grad

    copies = []
    for start in range(0, width, tile):
        span = slice(start, start + tile)
        total = jnp.zeros((columns, tile), jnp.float32)
        clip = 0
        for ref in grads:
            if len(ref.shape) == 2:
                total = total + squared(clip, ref[...], span)
                clip += 1
            else:
                total = lax.fori_loop(
                    0, ref.shape[0], lambda i, t, r=ref, s=span: t + squared(i, r[i], s), total
                )
                clip += ref.shape[0]
        fisher = total.T
        low_ref[span] = fisher.astype(low_ref.dtype)
        held[span] = fisher
        copies.append(
            pltpu.make_async_copy(
                held.at[span], own_ref.at[span, first : first + columns], done.at[len(copies)]
            )
        )
        copies[-1].start()
    for copy in copies:
        copy.wait()


def in_place(kernel, inputs, specs, previous, waits=()):
    extra = ([] if previous is None else [previous]) + list(waits)
    place = len(inputs)
    return (
        drop(kernel, place, len(extra)),
        list(inputs) + extra,
        list(specs) + [pl.BlockSpec(memory_space=pl.ANY)] * len(extra),
        {} if previous is None else {place: 0},
    )


def fisher_rows(rows, grads, first, total_columns, previous, waits):
    width = rows[0].shape[2]
    columns = grads[0].shape[-2]
    whole = pl.BlockSpec(memory_space=pltpu.VMEM)
    inputs = [*rows, *grads]
    kernel, inputs, specs, aliases = in_place(
        functools.partial(fisher_kernel, len(rows), first),
        inputs,
        [whole] * len(inputs),
        previous,
        waits,
    )
    return pl.pallas_call(
        kernel,
        in_specs=specs,
        out_specs=[pl.BlockSpec(memory_space=pl.ANY), whole],
        out_shape=[
            jax.ShapeDtypeStruct((width, total_columns), jnp.float32),
            jax.ShapeDtypeStruct((width, columns), jnp.bfloat16),
        ],
        scratch_shapes=[
            pltpu.VMEM((width, columns), jnp.float32),
            pltpu.SemaphoreType.DMA((width // row_tile(width),)),
        ],
        input_output_aliases=aliases,
        compiler_params=pltpu.CompilerParams(vmem_limit_bytes=FISHER_BYTES),
        name="fisher_rows",
    )(*inputs)


def merge_kernel(here_ref, there_ref, own_ref, other_ref, out_ref):
    zero = lax.axis_index("member") == 0
    here, there = to_f32(here_ref[...]) + damping, to_f32(there_ref[...]) + damping
    one, two = here * to_f32(own_ref[...]), there * to_f32(other_ref[...])
    upper = jnp.where(zero, one, two) + jnp.where(zero, two, one)
    out_ref[...] = upper / (here + there)


def merge_rows(here, there, own_weight, other_weight, first, offset, previous):
    width, columns = here.shape
    tile = width // 2
    plain = pl.BlockSpec((tile, columns), lambda i: (i, 0))
    part = pl.BlockSpec((pl.Element(tile), pl.Element(columns)), lambda i: (i * tile, first))
    other = pl.BlockSpec((pl.Element(tile), pl.Element(columns)), lambda i: (i * tile, offset))
    kernel, inputs, specs, aliases = in_place(
        merge_kernel, [here, there, own_weight, other_weight], [plain, plain, part, other], previous
    )
    return pl.pallas_call(
        kernel,
        grid=(width // tile,),
        in_specs=specs,
        out_specs=part,
        out_shape=jax.ShapeDtypeStruct(own_weight.shape, jnp.float32),
        input_output_aliases=aliases,
        compiler_params=pltpu.CompilerParams(vmem_limit_bytes=VMEM_BYTES),
        name="merge_rows",
    )(*inputs)


def spread_kernel(place_ref, rows_ref, *outs):
    rows = to_f32(rows_ref[...])
    average = jnp.mean(rows, axis=1, keepdims=True)
    centred = rows - average
    inverse = lax.rsqrt(jnp.mean(centred * centred, axis=1, keepdims=True) + 1e-06)
    size, width = len(outs), outs[0].shape[1]
    for away, out_ref in enumerate(outs):
        start = pl.multiple_of(lax.rem(place_ref[1] + away, size) * width, 128)
        part = to_f32(rows_ref[:, pl.ds(start, width)])
        out_ref[...] = ((part - average) * inverse).astype(out_ref.dtype)


def spread_rows(tokens, member, place, share, size):
    width = tokens.shape[1] // size
    return pl.pallas_call(
        spread_kernel,
        grid_spec=pltpu.PrefetchScalarGridSpec(
            num_scalar_prefetch=1,
            grid=(1,),
            in_specs=[pl.BlockSpec((share, tokens.shape[1]), lambda i, where: (where[0], 0))],
            out_specs=[pl.BlockSpec((share, width), lambda i, where: (0, 0))] * size,
        ),
        out_shape=[jax.ShapeDtypeStruct((share, width), jnp.bfloat16)] * size,
        compiler_params=pltpu.CompilerParams(vmem_limit_bytes=VMEM_BYTES),
        name="spread_rows",
    )(jnp.stack([member, place]).astype(jnp.int32), tokens)


def modulate(rows, modulation):
    return (rows * (1.0 + modulation[1:2]) + modulation[0:1]).astype(jnp.bfloat16)


def project_kernel(pieces, jobs, cuts, weights, waits, *refs):
    piece_refs, modulation_ref = refs[:pieces], refs[pieces]
    weight_refs = refs[pieces + 1 : pieces + 1 + weights]
    rows_ref, *outs = refs[pieces + 1 + weights + waits :]
    size = rows_ref.shape[0]
    share = piece_refs[0].shape[1]
    order = sorted(range(size), key=lambda away: -min(away, size - away))
    for away in order:
        modulation = modulation_ref[away]
        for i, ref in enumerate(piece_refs):
            rows_ref[away, i * share : (i + 1) * share] = modulate(to_f32(ref[away]), modulation)
        products = [
            jnp.dot(
                rows_ref[away, : count * share],
                weight_refs[index][...],
                preferred_element_type=jnp.float32,
            )
            for index, count in jobs
        ]
        products = products[0] if len(jobs) == 1 else jnp.concatenate(products, axis=0)
        products = products.astype(outs[0].dtype)
        middle = products.shape[0] // 2
        for part, (start, stop) in enumerate(zip(cuts[:-1], cuts[1:])):
            part_outs = outs[part * (size + 1) : (part + 1) * (size + 1)]
            if 2 * away == size:
                part_outs[away][...] = products[:middle, start:stop]
                part_outs[size][...] = products[middle:, start:stop]
            else:
                part_outs[away][...] = products[:, start:stop]


def project_rows(pieces, modulation, weights, jobs, cuts, waits):
    size, share, width = pieces[0].shape
    length = sum(count for _, count in jobs) * share
    lengths = [length // 2 if 2 * away == size else length for away in range(size)] + [length // 2]
    terms = [
        jax.ShapeDtypeStruct((lines, stop - start), jnp.bfloat16)
        for start, stop in zip(cuts[:-1], cuts[1:])
        for lines in lengths
    ]
    whole = pl.BlockSpec(memory_space=pltpu.VMEM)
    return pl.pallas_call(
        functools.partial(project_kernel, len(pieces), jobs, cuts, len(weights), len(waits)),
        in_specs=[whole] * (len(pieces) + 1 + len(weights))
        + [pl.BlockSpec(memory_space=pl.ANY)] * len(waits),
        out_specs=[pl.BlockSpec()] * (1 + len(terms)),
        out_shape=[jax.ShapeDtypeStruct((size, len(pieces) * share, width), jnp.bfloat16)] + terms,
        compiler_params=pltpu.CompilerParams(vmem_limit_bytes=VMEM_BYTES),
        name="project_rows",
    )(*pieces, modulation, *weights, *waits)


def to_f32(block):
    return block.astype(jnp.float32)


def added(term, message):
    return (to_f32(term) + to_f32(message)).astype(term.dtype)


def behind(*arrays):
    return lax.optimization_barrier(arrays)


class Ring:
    def __init__(self, size):
        self.size = size
        self.place = lax.axis_index("seq")
        self.short = size <= 8 and size % 2 == 0

    def by_distance(self, blocks):
        return jnp.take(blocks, (self.place - jnp.arange(self.size)) % self.size, axis=0)

    def step(self, block, away):
        pairs = [(i, (i + away) % self.size) for i in range(self.size)]
        return lax.ppermute(block, "seq", pairs)

    def exchange(self, tokens, member, share):
        size = self.size
        width = tokens.shape[1] // size
        if self.short and width % 128 == 0:
            parts = spread_rows(tokens, member, self.place, share, size)
            return jnp.stack(
                list(parts[:1]) + [self.step(part, away) for away, part in enumerate(parts) if away]
            )
        mine = to_f32(lax.dynamic_slice_in_dim(tokens, member * share, share, 0))
        centred = mine - jnp.mean(mine, axis=1, keepdims=True)
        variance = jnp.mean(centred * centred, axis=1, keepdims=True)
        normed = (centred * lax.rsqrt(variance + 1e-06)).astype(jnp.bfloat16)
        parts = normed.reshape(share, size, width)
        return self.by_distance(
            lax.all_to_all(parts, "seq", split_axis=1, concat_axis=0, tiled=False)
        )

    def project(self, pieces, modulation, weights, jobs, cuts, waits):
        size, half = self.size, self.size // 2
        if not self.short:
            share = pieces[0].shape[1]
            rows = jax.vmap(modulate)(to_f32(jnp.concatenate(pieces, axis=1)), modulation)
            terms = [
                jnp.einsum(
                    "crw,wn->crn",
                    rows[:, : count * share],
                    weights[index],
                    preferred_element_type=jnp.float32,
                ).astype(jnp.bfloat16)
                for index, count in jobs
            ]
            terms = jnp.concatenate(terms, axis=1)
            return rows, [(terms[:, :, a:b], ()) for a, b in zip(cuts[:-1], cuts[1:])]
        rows, *terms = project_rows(pieces, modulation, weights, jobs, cuts, waits)
        parts = []
        for part in range(len(cuts) - 1):
            own = terms[part * (size + 1) : (part + 1) * (size + 1)]
            parts.append((own, (self.step(own[half], 1), self.step(own[size], -1))))
        return rows, parts

    def sum(self, terms, first):
        size, half = self.size, self.size // 2
        if not self.short:
            return to_f32(lax.psum_scatter(self.by_distance(terms), "seq", tiled=False)), ()
        right, left = first
        middle = right.shape[0]
        for away in range(half - 1, 0, -1):
            term_right, term_left = terms[size - away], terms[away]
            if away == half - 1:
                term_right = jnp.concatenate(
                    [added(term_right[:middle], right), term_right[middle:]], axis=0
                )
                term_left = jnp.concatenate(
                    [term_left[:middle], added(term_left[middle:], left)], axis=0
                )
            else:
                term_right, term_left = added(term_right, right), added(term_left, left)
            right, left = self.step(term_right, 1), self.step(term_left, -1)
        if half == 1:
            return to_f32(terms[0]) + to_f32(jnp.concatenate([right, left], axis=0)), (right, left)
        return to_f32(terms[0]) + to_f32(right) + to_f32(left), (right, left)

    def spread(self, block):
        size, half = self.size, self.size // 2
        if not self.short:
            return [self.by_distance(lax.all_gather(block, "seq"))]
        blocks = [None] * size
        blocks[0] = block
        for away in range(1, half):
            blocks[away] = self.step(blocks[away - 1], 1)
            blocks[-away] = self.step(blocks[1 - away], -1)
        return blocks

    def complete(self, blocks, after):
        half = self.size // 2
        if not self.short:
            return blocks, blocks
        right, left = blocks[half - 1], blocks[(half + 1) % self.size]
        right, left = behind(right, left, *after)[:2]
        middle = right.shape[0] // 2
        last = [self.step(right[:middle], 1), self.step(left[middle:], -1)]
        return blocks[:half] + [jnp.concatenate(last, axis=0)] + blocks[half + 1 :], last


def on_device(
    axes, tokens, lattice, timestep, time_weight, query_weight, key_weight, values, cotangent
):
    members, clips, heads = axes
    member = lax.axis_index("member")
    clip = lax.axis_index("seq")
    head = lax.axis_index("head")
    own_query = query_weight[0]
    width, columns = own_query.shape
    share = tokens.shape[0] // members

    ring = Ring(clips)

    def x_swap(block):
        return lax.ppermute(block, "member", [(i, i ^ 1) for i in range(members)])

    def h_swap(block, bits):
        return lax.ppermute(block, "head", [(i, i ^ bits) for i in range(heads)])

    own = ring.exchange(tokens, member, share)

    ordered = timestep[(clip - jnp.arange(clips)) % clips]
    features = time_features(ordered, time_weight.shape[1])
    modulation = jnp.einsum(
        "cf,jfd->cjd", features, time_weight, preferred_element_type=jnp.float32
    )

    def both(block):
        return [block, h_swap(block, 1)]

    weights = [own_query, key_weight]
    head_count = columns // HEAD_SIZE
    last_heads = max(1, head_count // 5)
    bounds = [0, (head_count - last_heads) // 2, head_count - last_heads, head_count]
    cut = bounds[1] * HEAD_SIZE
    jobs, full = [(0, 2), (1, 2)], [0, columns]
    near_y, near_x = h_swap(own, 2), x_swap(own)
    rows_own, [(terms, first_own)] = ring.project(both(own), modulation, weights, jobs, full, [])
    sums_own, _ = ring.sum(terms, first_own)
    near_y, _ = behind(near_y, rows_own)
    far = x_swap(near_y)
    near_y = behind(near_y, *first_own)[0]
    rows_y, [(terms_y, first_y)] = ring.project(
        both(near_y), modulation, weights, jobs, full, [rows_own]
    )
    near_x, far, _ = behind(near_x, far, rows_y)
    rows_x, parts_x = ring.project(
        both(near_x) + both(far),
        modulation,
        [own_query],
        [(0, 4)],
        [0, cut, columns] if cut else full,
        [rows_y],
    )
    sums_y, _ = ring.sum(terms_y, behind(*first_y, rows_x)[:-1])
    lines = 2 * share
    key_here = jnp.concatenate([sums_own[lines:], sums_y[lines:]], axis=0)

    grid = lattice.reshape(3, 2, 2, members, share).transpose(0, 3, 1, 2, 4)
    for axis, bit in ((1, member), (2, head // 2), (3, head % 2)):
        grid = jnp.where(bit == 1, jnp.flip(grid, axis), grid)
    cosine, sine = rope_tables(grid.reshape(3, -1), HEAD_SIZE)

    pair = jnp.stack([values, cotangent[0]])
    blocks = []
    for bits in range(heads):
        block = lax.dynamic_slice_in_dim(pair, (head ^ bits) * columns, columns, 2)
        blocks.append(h_swap(block, bits) if bits else block)
    halves = jnp.stack(blocks, axis=1).reshape(2, heads, members, share, columns)
    halves = jnp.concatenate(
        [lax.dynamic_slice_in_dim(halves, member ^ i, 1, 2)[:, :, 0] for i in range(members)], axis=1
    ).reshape(2, members * heads * share, columns)
    value_rows, cot_rows = halves[0], halves[1]

    early, _ = behind(own_query[:, :cut], far)
    early = x_swap(early)

    rows_here = key_here.shape[0]
    key_here = rotate_heads(key_here, cosine[:rows_here], sine[:rows_here])
    key_here, early = behind(key_here, early, *parts_x[0][1])[:2]
    key_there = x_swap(key_here)
    key_rows = jnp.concatenate([key_here, key_there], axis=0)
    late, _ = behind(own_query[:, cut:], key_there)
    late = x_swap(late)

    queries, start = [], 0
    for terms, first in parts_x:
        query_x, _ = ring.sum(terms, first)
        span = slice(start, start + query_x.shape[1])
        queries.append(
            jnp.concatenate([sums_own[:lines, span], sums_y[:lines, span], query_x], axis=0)
        )
        start = span.stop

    operands = key_rows, value_rows, cot_rows, cosine.T, sine.T
    spans = [(first, last) for first, last in zip(bounds[:-1], bounds[1:]) if first < last]
    fisher, merged, lows, waits, ready = None, None, [], [], []
    for i, (first, last) in enumerate(spans):
        part = 1 if len(queries) > 1 and first * HEAD_SIZE >= cut else 0
        grad_query = attention_grad(
            queries[part], *operands, first - part * bounds[1], first, last - first, ready
        )
        blocks = ring.spread(behind(grad_query, *waits)[0] if i else grad_query)
        waits = [block for block in blocks[1:] if block is not None]
        ready = [grad_query] if i else [grad_query, *waits]
        blocks, far_blocks = ring.complete(blocks, lows[-1:])
        if i == 0:
            waits = [*far_blocks, late]
        first = first * HEAD_SIZE
        fisher, low = fisher_rows([rows_own, rows_y, rows_x], blocks, first, columns, fisher, [])
        lows.append(low)
        other, offset = (late, first - cut) if first >= cut else (early, first)
        merged = merge_rows(low, x_swap(low), own_query, other, first, offset, merged)
    return fisher[None], merged


def solution(mesh):
    axes = (mesh.shape["member"], mesh.shape["seq"], mesh.shape["head"])
    return jax.shard_map(
        functools.partial(on_device, axes),
        mesh=mesh,
        in_specs=(
            P(("seq", "head"), None),
            P(None, "seq"),
            P(),
            P(None, None, "seq"),
            P("member", "seq", "head"),
            P("seq", "head"),
            P(("seq", "head"), None),
            P("member", ("seq", "head"), None),
        ),
        out_specs=(P("member", "seq", "head"), P("seq", "head")),
        check_vma=False,
    )
```
